32 devices in a mesh: sec: 4 (over z), row: 4 (over y, core), rad: 2 (over x).
Axes of the slice: x: 2, y: 2, z: 4, core: 2. Of those that a mesh axis runs over, the one named last changes fastest.
Arguments:
- state: float32 [5, 4, 16, 16, 512], P(None, 'sec', None, 'rad', 'row'), may hold values from -6 to 6
- volume: float32 [4, 16, 16, 512], P('sec', None, 'rad', 'row'), may hold values from 0.5 to 2
- face_axial: float32 [4, 16, 16, 512], P('sec', None, 'rad', 'row'), may hold values from 0.5 to 1.5
- face_radial: float32 [4, 16, 16, 512], P('sec', None, 'rad', 'row'), may hold values from 0.5 to 1.5
- face_circum: float32 [4, 16, 16, 512], P('sec', None, 'rad', 'row'), may hold values from 0.5 to 1.5
- viscosity: float32 [4, 16, 16, 512], P('sec', None, 'rad', 'row'), may hold values from 0.05 to 0.5
- flux_matrix: float32 [4, 3, 5, 5], P('sec'), may hold values from -2.5 to 2.5
- inflow_plane: float32 [5, 16, 512], P(None, 'rad', 'row'), may hold values from -6 to 6
- outflow_plane: float32 [5, 16, 512], P(None, 'rad', 'row'), may hold values from -6 to 6
- down_donors: int32 [4, 64], P('sec', ('row', 'rad')), may hold values from 0 to 63, each once within a row
- up_donors: int32 [4, 64], P('sec', ('row', 'rad')), may hold values from 0 to 63, each once within a row
- pressure_weight: float32 [5], replicated, may hold values from -3 to 3
- boundary_coupling: float32 [5], replicated, may hold values from -4 to 4
Outputs:
- advanced: float32 [5, 4, 16, 16, 512], P(None, 'sec', None, 'rad', 'row')
The draws below stay inside these ranges and needn't reach their ends.
Inputs may be any that keep to these rules, and one draw needn't show every extreme that they name: `down_donors`: each row names each of the 64 tiles exactly once. `up_donors`: each row names each of the 64 tiles exactly once.
All inputs are finite; a program needn't handle non-finite values.
Results may differ from the reference program's by a relative error of at most 0.0001.
Values sent between devices are 32-bit elements; how exact they have to be, the bound alone decides.
A program may use at most 64 MiB of HBM per device.

```python
import math
import jax
import jax.numpy as jnp
from jax import lax

NV = 5
STEPS = 4
CX = 16
CR = 8
CC = 128
NT = 64
NR = 16
NC = 512
N_SEC = 4
N_ROW = 4
N_RAD = 2


def level_of(stream_key, shape, shards, low, high):
    loudness, own = 1.0, jax.random.fold_in(stream_key, 6)
    for dim, blocks in shards:
        steps = jnp.exp(jax.random.uniform(jax.random.fold_in(own, dim), (blocks,), jnp.float32, low / len(shards), high / len(shards)))
        loudness = loudness * jnp.repeat(steps, shape[dim] // blocks).reshape([-1 if axis == dim else 1 for axis in range(len(shape))])
    return loudness


def bell_draw(rng, dims, deviation, reach, split=(), kind=jnp.bfloat16):
    array = deviation * jax.random.normal(rng, dims, jnp.float32)
    if split:
        array = array * level_of(rng, dims, split, -0.22, 0.18)
    return jnp.clip(array, -reach, reach).astype(kind)


def setup_inputs(seed: int = 0) -> dict:
    key_list = jax.random.split(jax.random.key(seed), 14)
    return {
        "state": bell_draw(key_list[0], (NV, N_SEC, CX, NR, NC), 1.0, 6.0, ((1, 4), (3, 2), (4, 4)), jnp.float32),
        "volume": jnp.clip(jnp.exp(math.log(2.0) - 1.3862944 * jax.random.uniform(key_list[1], (N_SEC, CX, NR, NC), jnp.float32) ** level_of(key_list[1], (N_SEC, CX, NR, NC), ((0, 4), (2, 2), (3, 4)), -0.2, 0.2)), 0.5, 2.0),
        "face_axial": jnp.clip(jnp.exp(math.log(1.5) - 1.0986123 * jax.random.uniform(key_list[2], (N_SEC, CX, NR, NC), jnp.float32) ** level_of(key_list[2], (N_SEC, CX, NR, NC), ((0, 4), (2, 2), (3, 4)), -0.2, 0.2)), 0.5, 1.5),
        "face_radial": jnp.clip(jnp.exp(math.log(1.5) - 1.0986123 * jax.random.uniform(key_list[3], (N_SEC, CX, NR, NC), jnp.float32) ** level_of(key_list[3], (N_SEC, CX, NR, NC), ((0, 4), (2, 2), (3, 4)), -0.2, 0.2)), 0.5, 1.5),
        "face_circum": jnp.clip(jnp.exp(math.log(1.5) - 1.0986123 * jax.random.uniform(key_list[4], (N_SEC, CX, NR, NC), jnp.float32) ** level_of(key_list[4], (N_SEC, CX, NR, NC), ((0, 4), (2, 2), (3, 4)), -0.2, 0.2)), 0.5, 1.5),
        "viscosity": jnp.clip(jnp.exp(math.log(0.5) - 2.3025851 * jax.random.uniform(key_list[5], (N_SEC, CX, NR, NC), jnp.float32) ** level_of(key_list[5], (N_SEC, CX, NR, NC), ((0, 4), (2, 2), (3, 4)), -0.2, 0.2)), 0.05, 0.5),
        "flux_matrix": bell_draw(key_list[6], (N_SEC, 3, NV, NV), NV ** -0.5, 2.5, ((0, 4),), jnp.float32),
        "inflow_plane": bell_draw(key_list[7], (NV, NR, NC), 1.0, 6.0, ((1, 2), (2, 4)), jnp.float32),
        "outflow_plane": bell_draw(key_list[8], (NV, NR, NC), 1.0, 6.0, ((1, 2), (2, 4)), jnp.float32),
        "down_donors": jax.vmap(lambda own: jax.random.permutation(own, NT))(jax.random.split(key_list[9], N_SEC)).reshape((N_SEC, NT)).astype(jnp.int32),
        "up_donors": jax.vmap(lambda own: jax.random.permutation(own, NT))(jax.random.split(key_list[10], N_SEC)).reshape((N_SEC, NT)).astype(jnp.int32),
        "pressure_weight": bell_draw(key_list[11], (NV,), 0.5, 3.0, (), jnp.float32),
        "boundary_coupling": bell_draw(key_list[12], (NV,), 1.0, 4.0, (), jnp.float32),
    }


time_step = 0.08


def to_tiles(plane):
    components = plane.shape[0]
    shaped = plane.reshape(components, N_RAD, CR, N_ROW, CC // 128, 128)
    return shaped.transpose(3, 1, 2, 4, 0, 5).reshape(NT, components, 128)


def from_tiles(tiles):
    components = tiles.shape[1]
    shaped = tiles.reshape(N_ROW, N_RAD, CR, CC // 128, components, 128)
    return shaped.transpose(4, 1, 2, 0, 3, 5).reshape(components, NR, NC)


def face_divergence(padded, face_area, viscous, matrix, direction):
    length = padded.shape[direction]
    lower_cells = lax.slice_in_dim(padded, 0, length - 1, axis=direction)
    upper_cells = lax.slice_in_dim(padded, 1, length, axis=direction)
    mixed = jnp.einsum("uv,v...->u...", matrix, lower_cells + upper_cells, precision=lax.Precision.HIGHEST)
    fluxes = face_area * (0.5 * mixed - viscous * (upper_cells - lower_cells))
    return lax.slice_in_dim(fluxes, 1, length - 1, axis=direction) - lax.slice_in_dim(fluxes, 0, length - 2, axis=direction)


def pressure_of(weights, plane):
    return jnp.einsum("v,vjk->jk", weights, plane, precision=lax.Precision.HIGHEST)


def reference(state, volume, face_axial, face_radial, face_circum, viscosity, flux_matrix, inflow_plane, outflow_plane, down_donors, up_donors, pressure_weight, boundary_coupling):
    sections = [state[:, section_id] for section_id in range(N_SEC)]
    for step_index in range(STEPS):
        fresh = []
        for section_id in range(N_SEC):
            field = sections[section_id]
            if section_id == 0:
                donor = inflow_plane
            else:
                donor = sections[section_id - 1][:, -1]
            if section_id == N_SEC - 1:
                beyond = outflow_plane
            else:
                beyond = sections[section_id + 1][:, 0]
            inlet_ghost = from_tiles(jnp.take(to_tiles(donor), down_donors[section_id], axis=0))
            beyond_pressure = pressure_of(pressure_weight, beyond)[None]
            mapped = from_tiles(jnp.take(to_tiles(beyond_pressure), up_donors[section_id], axis=0))[0]
            outlet = field[:, -1]
            outlet_ghost = outlet + boundary_coupling[:, None, None] * (mapped - pressure_of(pressure_weight, outlet))[None]
            axial_padded = jnp.concatenate([inlet_ghost[:, None], field, outlet_ghost[:, None]], axis=1)
            own_face = face_axial[section_id]
            axial_area = jnp.concatenate([own_face[:1], own_face], axis=0)
            own_mu = viscosity[section_id]
            mu_axial = jnp.concatenate([own_mu[:1], own_mu, own_mu[-1:]], axis=0)
            nu_axial = 0.5 * (mu_axial[:-1] + mu_axial[1:])
            radial_face = face_radial[section_id]
            radial_face = jnp.concatenate([radial_face[:, :-1], jnp.zeros_like(radial_face[:, -1:])], axis=1)
            radial_area = jnp.concatenate([radial_face[:, -1:], radial_face], axis=1)
            mu_radial = jnp.pad(own_mu, ((0, 0), (1, 1), (0, 0)), mode="wrap")
            nu_radial = 0.5 * (mu_radial[:, :-1] + mu_radial[:, 1:])
            radial_padded = jnp.pad(field, ((0, 0), (0, 0), (1, 1), (0, 0)), mode="wrap")
            circ_face = face_circum[section_id]
            circ_area = jnp.concatenate([circ_face[:, :, -1:], circ_face], axis=2)
            mu_circ = jnp.pad(own_mu, ((0, 0), (0, 0), (1, 1)), mode="wrap")
            nu_circ = 0.5 * (mu_circ[:, :, :-1] + mu_circ[:, :, 1:])
            circ_padded = jnp.pad(field, ((0, 0), (0, 0), (0, 0), (1, 1)), mode="wrap")
            divergence = face_divergence(axial_padded, axial_area, nu_axial, flux_matrix[section_id, 0], 1)
            divergence = divergence + face_divergence(radial_padded, radial_area, nu_radial, flux_matrix[section_id, 1], 2)
            divergence = divergence + face_divergence(circ_padded, circ_area, nu_circ, flux_matrix[section_id, 2], 3)
            fresh.append(field - (time_step / volume[section_id]) * divergence)
        sections = fresh
    return jnp.stack(sections, axis=1)
```

```python
import functools

import jax
import jax.numpy as jnp
from jax import lax
from jax.experimental import pallas as pl
from jax.experimental.pallas import tpu as pltpu
from jax.sharding import PartitionSpec as P

STEPS = 4


time_step = 0.08

MESH = pl.DeviceIdType.MESH
N_COEF = 16


def kernel(
    sizes,
    state,
    volume,
    face_axial,
    face_radial,
    face_circum,
    viscosity,
    matrix,
    inflow,
    outflow,
    down,
    up,
    weight,
    coupling,
    out,
    field,
    coef,
    flow,
    flow_send,
    press,
    press_send,
    ghost,
    mapped,
    row_in,
    row_out,
    rad_in,
    rad_out,
    rad_in0,
    rad_out0,
    flow_ss,
    flow_rs,
    press_ss,
    press_rs,
    edge_ss,
    row_ss,
    row_rs,
    rad_ss,
    rad_rs,
):
    n_sec, n_row, n_rad, nv, nx, nr, lanes = sizes
    group = n_row * n_rad
    planes = nv * nx
    block = nv * nr
    sec, row, rad = lax.axis_index("sec"), lax.axis_index("row"), lax.axis_index("rad")
    mine = row * n_rad + rad
    first, last = sec == 0, sec == n_sec - 1
    floor, casing = rad == 0, rad == n_rad - 1
    right, left = lax.rem(row + 1, n_row), lax.rem(row + n_row - 1, n_row)
    lane = lax.broadcasted_iota(jnp.int32, (nr, lanes), 1)
    sub = lax.broadcasted_iota(jnp.int32, (nr, lanes), 0)

    def device(section, index):
        return {"sec": section, "row": lax.div(index, n_rad), "rad": lax.rem(index, n_rad)}

    def each(action, skip_self=False):
        def one(i):
            index = lax.rem(mine + i, group)
            action(index)

        start = 1 if skip_self else 0
        if group <= 16:
            for i in range(start, group):
                one(i)
        else:
            pl.loop(start, group)(one)

    def send(src, dst, send_sem, recv_sem, to):
        pltpu.make_async_remote_copy(
            src_ref=src,
            dst_ref=dst,
            send_sem=send_sem,
            recv_sem=recv_sem,
            device_id=to,
            device_id_type=MESH,
        ).start()

    def wait(ref, sem):
        pltpu.make_async_copy(ref, ref, sem).wait()

    def rows(index):
        if isinstance(index, int):
            return pl.ds(index * nr, nr)
        return pl.ds(pl.multiple_of(index * nr, nr), nr)

    barrier = pltpu.get_barrier_semaphore()

    def greet(to):
        pl.semaphore_signal(barrier, inc=1, device_id=to, device_id_type=MESH)

    greet({"row": left})
    greet({"row": right})

    @pl.when(jnp.logical_not(floor))
    def _():
        greet({"rad": rad - 1})

    @pl.when(jnp.logical_not(casing))
    def _():
        greet({"rad": rad + 1})

    @pl.when(jnp.logical_not(first))
    def _():
        each(lambda index: greet(device(sec - 1, index)))

    @pl.when(jnp.logical_not(last))
    def _():
        each(lambda index: greet(device(sec + 1, index)))

    @pl.when(first)
    def _():
        each(lambda index: greet(device(sec, index)), True)

    @pl.when(last)
    def _():
        each(lambda index: greet(device(sec, index)), True)

    def pressure_of(values):
        total = weight[0] * values[0]
        for v in range(1, nv):
            total = total + weight[v] * values[v]
        return total

    press_send[0] = pressure_of([state[rows(v * nx)] for v in range(nv)])
    press_send[STEPS] = pressure_of([outflow[rows(v)] for v in range(nv)])
    for v in range(nv):
        flow_send[0, rows(v)] = state[rows(v * nx + nx - 1)]

    def pack_one(packs, value, index):
        to_left, to_right = packs
        to_left = jnp.where(lane == index, pltpu.roll(value, index, 1), to_left)
        to_right = jnp.where(lane == index, pltpu.roll(value, index + 1, 1), to_right)
        return to_left, to_right

    blank = jnp.zeros((nr, lanes), jnp.float32)

    def pack_start(x, packs):
        for v in range(nv):
            packs = pack_one(packs, state[rows(v * nx + x)], v * nx + x)
        packs = pack_one(packs, viscosity[rows(x)], planes + x)
        return pack_one(packs, face_circum[rows(x)], planes + nx + x)

    packs = lax.fori_loop(0, nx, pack_start, (blank, blank))
    row_out[0, 0, 0] = packs[0]
    row_out[0, 0, 1] = packs[1]
    for side, edge in ((0, 0), (1, nr - 1)):
        rad_out[0, side, pl.ds(0, planes)] = state[pl.ds(edge, planes, stride=nr)]
        rad_out[0, side, pl.ds(planes, nx)] = viscosity[pl.ds(edge, nx, stride=nr)]
        rad_out[0, side, pl.ds(planes + nx, nx)] = face_radial[pl.ds(edge, nx, stride=nr)]
    for v in range(nv):
        for slot in range(2):
            field[slot, rows(v * nx)] = blank
    for step in range(STEPS):
        for side in range(2):
            rad_out0[step, side] = blank

    @pl.when(floor)
    def _():
        for step in range(STEPS):
            rad_in[step, 0] = jnp.zeros(rad_in.shape[2:], jnp.float32)
            rad_in0[step, 0] = blank

    @pl.when(casing)
    def _():
        for step in range(STEPS):
            rad_in[step, 1] = jnp.zeros(rad_in.shape[2:], jnp.float32)
            rad_in0[step, 1] = blank

    one = jnp.int32(1)
    zero = jnp.int32(0)
    inner = group + group - jnp.where(jnp.logical_or(first, last), one, zero)
    inner = inner - (1 if n_sec == 1 else 0)
    beside = jnp.where(floor, zero, one) + jnp.where(casing, zero, one)
    pl.semaphore_wait(barrier, 2 + inner + beside)

    def send_flow(step):
        @pl.when(jnp.logical_not(last))
        def _():
            each(
                lambda index: send(
                    flow_send.at[step],
                    flow[step].at[mine],
                    flow_ss.at[step],
                    flow_rs.at[step],
                    device(sec + 1, index),
                )
            )

    def send_press(step):
        @pl.when(jnp.logical_not(first))
        def _():
            each(
                lambda index: send(
                    press_send.at[step],
                    press[step].at[mine],
                    press_ss.at[step],
                    press_rs.at[step],
                    device(sec - 1, index),
                )
            )

    def send_rows(step, part):
        for side, to in ((0, left), (1, right)):
            send(
                row_out.at[step, part, side],
                row_in.at[step, part, 1 - side],
                row_ss.at[step, part, side],
                row_rs.at[step, part, 1 - side],
                {"row": to},
            )

    def rad_refs(step, part, side):
        if part:
            return rad_out0.at[step, side], rad_in0.at[step, 1 - side]
        count = planes if step else planes + 2 * nx
        return (
            rad_out.at[step, side, pl.ds(0, count)],
            rad_in.at[step, 1 - side, pl.ds(0, count)],
        )

    def send_rads(step, part):
        for side, edge, to in ((0, floor, rad - 1), (1, casing, rad + 1)):

            @pl.when(jnp.logical_not(edge))
            def _(side=side, to=to):
                src, dst = rad_refs(step, part, side)
                send(
                    src,
                    dst,
                    rad_ss.at[step, part, side],
                    rad_rs.at[step, part, 1 - side],
                    {"rad": to},
                )

    def wait_beside(step, part):
        for side, edge in ((0, floor), (1, casing)):
            wait(row_in.at[step, part, side], row_rs.at[step, part, side])

            @pl.when(jnp.logical_not(edge))
            def _(side=side):
                wait(rad_refs(step, part, 1 - side)[1], rad_rs.at[step, part, side])

    send_rows(0, 0)
    send_rads(0, 0)
    send_press(0)

    @pl.when(last)
    def _():
        each(
            lambda index: send(
                press_send.at[STEPS],
                press[0].at[mine],
                edge_ss.at[1],
                press_rs.at[0],
                device(sec, index),
            ),
            True,
        )
        pltpu.make_async_copy(press_send.at[STEPS], press[0].at[mine], press_rs.at[0]).start()

    @pl.when(first)
    def _():
        each(
            lambda index: send(
                inflow, flow[0].at[mine], edge_ss.at[0], flow_rs.at[0], device(sec, index)
            ),
            True,
        )
        pltpu.make_async_copy(inflow, flow[0].at[mine], flow_rs.at[0]).start()

    send_flow(0)

    wait_beside(0, 0)

    def lower_lane(value, packed, index):
        return jnp.where(
            lane == 0, pltpu.roll(packed, lax.rem(lanes - index, lanes), 1), pltpu.roll(value, 1, 1)
        )

    def upper_lane(value, packed, index):
        return jnp.where(
            lane == lanes - 1,
            pltpu.roll(packed, lanes - 1 - index, 1),
            pltpu.roll(value, lanes - 1, 1),
        )

    def lower_sub(value, edge_row):
        return jnp.where(sub == 0, edge_row, pltpu.roll(value, 1, 0))

    def upper_sub(value, edge_row):
        return jnp.where(sub == nr - 1, edge_row, pltpu.roll(value, nr - 1, 0))

    wall = jnp.logical_and(casing, sub == nr - 1)

    def prepare(x, carry):
        below, above = jnp.maximum(x - 1, 0), jnp.minimum(x + 1, nx - 1)
        scale = time_step / volume[rows(x)]
        half = 0.5 * scale
        mu = viscosity[rows(x)]
        area = face_radial[rows(x)]
        area = jnp.where(wall, 0.0, area)
        around = face_circum[rows(x)]
        from_left, from_right = row_in[0, 0, 0], row_in[0, 0, 1]
        lower = (
            (face_axial[rows(below)], viscosity[rows(below)]),
            (
                lower_sub(area, rad_in[0, 0, pl.ds(planes + nx + x, 1)]),
                lower_sub(mu, rad_in[0, 0, pl.ds(planes + x, 1)]),
            ),
            (
                lower_lane(around, from_left, planes + nx + x),
                lower_lane(mu, from_left, planes + x),
            ),
        )
        upper = (
            (face_axial[rows(x)], viscosity[rows(above)]),
            (area, upper_sub(mu, rad_in[0, 1, pl.ds(planes + x, 1)])),
            (around, upper_lane(mu, from_right, planes + x)),
        )
        keep = jnp.ones_like(mu)
        for d in range(3):
            area_l, mu_l = lower[d]
            area_u, mu_u = upper[d]
            mix_l, mix_u = half * area_l, half * area_u
            spread_l, spread_u = mix_l * (mu_l + mu), mix_u * (mu_u + mu)
            keep = keep - (spread_l + spread_u)
            coef[5 * d, rows(x)] = mix_u
            coef[5 * d + 1, rows(x)] = mix_u - mix_l
            coef[5 * d + 2, rows(x)] = mix_l
            coef[5 * d + 3, rows(x)] = spread_u
            coef[5 * d + 4, rows(x)] = spread_l
        coef[N_COEF - 1, rows(x)] = keep
        return carry

    lax.fori_loop(0, nx, prepare, 0)

    def advance(x, centre, before, after, packed, edge_rows):
        from_left, from_right = packed
        c = [coef[k, rows(x)] for k in range(N_COEF)]
        mixed, fresh = [], []
        for v in range(nv):
            index = v * nx + x
            mid = centre[v]
            below, above = edge_rows(v)
            pairs = (
                (before[v], after[v]),
                (lower_sub(mid, below), upper_sub(mid, above)),
                (lower_lane(mid, from_left, index), upper_lane(mid, from_right, index)),
            )
            kept = c[N_COEF - 1] * mid
            for d, (lo, hi) in enumerate(pairs):
                mixed.append(c[5 * d] * hi + c[5 * d + 1] * mid - c[5 * d + 2] * lo)
                kept = kept + (c[5 * d + 3] * hi + c[5 * d + 4] * lo)
            fresh.append(kept)
        result = []
        for u in range(nv):
            total = None
            for d in range(3):
                for v in range(nv):
                    term = matrix[0, d, u, v] * mixed[3 * v + d]
                    total = term if total is None else total + term
            result.append(fresh[u] - total)
        return result

    for step in range(STEPS):
        final = step == STEPS - 1
        src = state if step == 0 else field.at[(step - 1) % 2]
        dst = out if final else field.at[step % 2]
        if step:
            wait_beside(step, 0)

        def plane(x):
            return [src[rows(v * nx + x)] for v in range(nv)]

        def keep_plane(x, values):
            for v in range(nv):
                dst[rows(v * nx + x)] = values[v]

        def pack_plane(x, values, packs):
            if final:
                return packs
            for v in range(nv):
                packs = pack_one(packs, values[v], v * nx + x)
            return packs

        def edge_rows_at(x, step=step):
            def edge_rows(v):
                at = pl.ds(v * nx + x, 1)
                return rad_in[step, 0, at], rad_in[step, 1, at]

            return edge_rows

        def inside(x, packs):
            packed = row_in[step, 0, 0], row_in[step, 0, 1]
            values = advance(
                x, plane(x), plane(x - 1), plane(x + 1), packed, edge_rows_at(x)
            )
            keep_plane(x, values)
            return pack_plane(x, values, packs)

        def inside_two(i, packs):
            x = 1 + 2 * i
            return inside(x + 1, inside(x, packs))

        pairs = (nx - 2) // 2
        packs = lax.fori_loop(0, pairs, inside_two, (blank, blank))
        for x in range(1 + 2 * pairs, nx - 1):
            packs = inside(x, packs)

        def take_press(step=step):
            wait(press[step], press_rs.at[step])
            for a in range(nr):
                donor = up[0, a]
                at = pl.ds(lax.rem(donor, nr), 1)
                mapped[pl.ds(a, 1)] = press[step][lax.div(donor, nr), at]

        if step:
            pl.when(jnp.logical_not(last))(take_press)
        else:
            take_press()
        centre = plane(nx - 1)
        gap = mapped[...] - pressure_of(centre)
        after = [centre[v] + coupling[v] * gap for v in range(nv)]
        packed = row_in[step, 0, 0], row_in[step, 0, 1]
        values = advance(
            nx - 1, centre, plane(nx - 2), after, packed, edge_rows_at(nx - 1)
        )
        keep_plane(nx - 1, values)
        if not final:
            for v in range(nv):
                flow_send[step + 1, rows(v)] = values[v]
            send_flow(step + 1)
            packs = pack_plane(nx - 1, values, packs)
            row_out[step + 1, 0, 0] = packs[0]
            row_out[step + 1, 0, 1] = packs[1]
            send_rows(step + 1, 0)
            for side, edge in ((0, 0), (1, nr - 1)):
                rad_out[step + 1, side, pl.ds(0, planes)] = dst[pl.ds(edge, planes, stride=nr)]
            send_rads(step + 1, 0)

        def take_flow(step=step):
            wait(flow[step], flow_rs.at[step])
            for a in range(nr):
                donor = down[0, a]
                owner, base = lax.div(donor, nr), lax.rem(donor, nr)
                for v in range(nv):
                    ghost[pl.ds(v * nr + a, 1)] = flow[step][owner, pl.ds(v * nr + base, 1)]

        if step:
            wait_beside(step, 1)
            pl.when(jnp.logical_not(first))(take_flow)

            def edge_rows(v, step=step):
                at = pl.ds(v, 1)
                return rad_in0[step, 0, at], rad_in0[step, 1, at]

            packed = row_in[step, 1, 0], row_in[step, 1, 1]
        else:
            take_flow()
            edge_rows = edge_rows_at(0)
        before = [ghost[rows(v)] for v in range(nv)]
        values = advance(0, plane(0), before, plane(1), packed, edge_rows)
        keep_plane(0, values)
        if not final:
            press_send[step + 1] = pressure_of(values)
            send_press(step + 1)
            packs = pack_plane(0, values, (blank, blank))
            row_out[step + 1, 1, 0] = packs[0]
            row_out[step + 1, 1, 1] = packs[1]
            send_rows(step + 1, 1)
            for v in range(nv):
                rad_out0[step + 1, 0, pl.ds(v, 1)] = values[v][:1]
                rad_out0[step + 1, 1, pl.ds(v, 1)] = values[v][nr - 1 :]
            send_rads(step + 1, 1)

    for step in range(STEPS):
        for part in range(2 if step else 1):
            for side, edge in ((0, floor), (1, casing)):
                wait(row_out.at[step, part, side], row_ss.at[step, part, side])

                @pl.when(jnp.logical_not(edge))
                def _(step=step, part=part, side=side):
                    wait(rad_refs(step, part, side)[0], rad_ss.at[step, part, side])

    @pl.when(jnp.logical_not(last))
    def _():
        for step in range(STEPS):
            wait(flow[step], flow_ss.at[step])

    @pl.when(jnp.logical_not(first))
    def _():
        for step in range(STEPS):
            wait(press[step], press_ss.at[step])

    @pl.when(first)
    def _():
        wait(flow[0].at[pl.ds(0, group - 1)], edge_ss.at[0])

    @pl.when(last)
    def _():
        wait(press[0].at[pl.ds(0, group - 1)], edge_ss.at[1])


def body(
    n_sec,
    n_row,
    n_rad,
    state,
    volume,
    face_axial,
    face_radial,
    face_circum,
    viscosity,
    flux_matrix,
    inflow_plane,
    outflow_plane,
    down_donors,
    up_donors,
    pressure_weight,
    boundary_coupling,
):
    nv, _, nx, nr, lanes = state.shape
    group = n_row * n_rad
    planes, block = nv * nx, nv * nr
    held = planes + 2 * nx

    def flat(array):
        return array.reshape(-1, lanes)

    def vmem(*shape):
        return pltpu.VMEM(shape, jnp.float32)

    dma = pltpu.SemaphoreType.DMA
    in_vmem = pl.BlockSpec(memory_space=pltpu.VMEM)
    in_smem = pl.BlockSpec(memory_space=pltpu.SMEM)
    result = pl.pallas_call(
        functools.partial(kernel, (n_sec, n_row, n_rad, nv, nx, nr, lanes)),
        out_shape=jax.ShapeDtypeStruct((planes * nr, lanes), jnp.float32),
        in_specs=[in_vmem] * 6 + [in_smem] + [in_vmem] * 2 + [in_smem] * 4,
        out_specs=in_vmem,
        scratch_shapes=[
            vmem(2, planes * nr, lanes),
            vmem(N_COEF, nx * nr, lanes),
            [vmem(group, block, lanes)] * STEPS,
            vmem(STEPS, block, lanes),
            [vmem(group, nr, lanes)] * STEPS,
            vmem(STEPS + 1, nr, lanes),
            vmem(block, lanes),
            vmem(nr, lanes),
            vmem(STEPS, 2, 2, nr, lanes),
            vmem(STEPS, 2, 2, nr, lanes),
            vmem(STEPS, 2, held, lanes),
            vmem(STEPS, 2, held, lanes),
            vmem(STEPS, 2, nr, lanes),
            vmem(STEPS, 2, nr, lanes),
            dma((STEPS,)),
            dma((STEPS,)),
            dma((STEPS,)),
            dma((STEPS,)),
            dma((2,)),
            dma((STEPS, 2, 2)),
            dma((STEPS, 2, 2)),
            dma((STEPS, 2, 2)),
            dma((STEPS, 2, 2)),
        ],
        compiler_params=pltpu.CompilerParams(
            collective_id=0, has_side_effects=True, vmem_limit_bytes=32 * 1024 * 1024
        ),
        name="coupled_steps",
    )(
        flat(state),
        flat(volume),
        flat(face_axial),
        flat(face_radial),
        flat(face_circum),
        flat(viscosity),
        flux_matrix,
        flat(inflow_plane),
        flat(outflow_plane),
        down_donors,
        up_donors,
        pressure_weight,
        boundary_coupling,
    )
    return result.reshape(state.shape)


def solution(mesh):
    in_specs = (
        P(None, "sec", None, "rad", "row"),
        P("sec", None, "rad", "row"),
        P("sec", None, "rad", "row"),
        P("sec", None, "rad", "row"),
        P("sec", None, "rad", "row"),
        P("sec", None, "rad", "row"),
        P("sec", None, None, None),
        P(None, "rad", "row"),
        P(None, "rad", "row"),
        P("sec", ("row", "rad")),
        P("sec", ("row", "rad")),
        P(),
        P(),
    )
    out_specs = P(None, "sec", None, "rad", "row")
    sizes = tuple(mesh.shape[name] for name in ("sec", "row", "rad"))
    return jax.shard_map(
        functools.partial(body, *sizes),
        mesh=mesh,
        in_specs=in_specs,
        out_specs=out_specs,
        check_vma=False,
    )
```

```python
import functools

import jax
import jax.numpy as jnp
from jax import lax
from jax.experimental import pallas as pl
from jax.experimental.pallas import tpu as pltpu
from jax.sharding import PartitionSpec as P

STEPS = 4


time_step = 0.08

MESH = pl.DeviceIdType.MESH
N_COEF = 16


def kernel(
    sizes,
    state_hbm,
    volume_hbm,
    face_axial_hbm,
    face_radial_hbm,
    face_circum_hbm,
    viscosity_hbm,
    matrix_hbm,
    inflow,
    outflow_hbm,
    down_hbm,
    up_hbm,
    weight_hbm,
    coupling_hbm,
    out,
    state,
    volume,
    face_axial,
    face_radial,
    face_circum,
    viscosity,
    matrix,
    outflow,
    down,
    up,
    weight,
    coupling,
    loaded,
    field,
    coef,
    flow,
    flow_send,
    press,
    press_send,
    ghost,
    mapped,
    row_in,
    row_out,
    rad_in,
    rad_out,
    rad_in0,
    rad_out0,
    flow_ss,
    flow_rs,
    press_ss,
    press_rs,
    edge_ss,
    row_ss,
    row_rs,
    rad_ss,
    rad_rs,
):
    n_sec, n_row, n_rad, nv, nx, nr, lanes = sizes
    group = n_row * n_rad
    planes = nv * nx
    block = nv * nr
    sec, row, rad = lax.axis_index("sec"), lax.axis_index("row"), lax.axis_index("rad")
    mine = row * n_rad + rad
    first, last = sec == 0, sec == n_sec - 1
    floor, casing = rad == 0, rad == n_rad - 1
    right, left = lax.rem(row + 1, n_row), lax.rem(row + n_row - 1, n_row)
    lane = lax.broadcasted_iota(jnp.int32, (nr, lanes), 1)
    sub = lax.broadcasted_iota(jnp.int32, (nr, lanes), 0)

    def device(section, index):
        return {"sec": section, "row": lax.div(index, n_rad), "rad": lax.rem(index, n_rad)}

    def each(action, skip_self=False):
        def one(i):
            index = lax.rem(mine + i, group)
            action(index)

        start = 1 if skip_self else 0
        if group <= 16:
            for i in range(start, group):
                one(i)
        else:
            pl.loop(start, group)(one)

    def send(src, dst, send_sem, recv_sem, to):
        pltpu.make_async_remote_copy(
            src_ref=src,
            dst_ref=dst,
            send_sem=send_sem,
            recv_sem=recv_sem,
            device_id=to,
            device_id_type=MESH,
        ).start()

    def wait(ref, sem):
        pltpu.make_async_copy(ref, ref, sem).wait()

    def rows(index):
        if isinstance(index, int):
            return pl.ds(index * nr, nr)
        return pl.ds(pl.multiple_of(index * nr, nr), nr)

    loads = [
        pltpu.make_async_copy(src, dst, loaded.at[i])
        for i, (src, dst) in enumerate(
            (
                (state_hbm, state),
                (viscosity_hbm, viscosity),
                (face_circum_hbm, face_circum),
                (face_radial_hbm, face_radial),
                (weight_hbm, weight),
                (outflow_hbm, outflow),
                (volume_hbm, volume),
                (face_axial_hbm, face_axial),
                (up_hbm, up),
                (coupling_hbm, coupling),
                (matrix_hbm, matrix),
                (down_hbm, down),
            )
        )
    ]
    for load in loads:
        load.start()

    barrier = pltpu.get_barrier_semaphore()

    def greet(to):
        pl.semaphore_signal(barrier, inc=1, device_id=to, device_id_type=MESH)

    greet({"row": left})
    greet({"row": right})

    @pl.when(jnp.logical_not(floor))
    def _():
        greet({"rad": rad - 1})

    @pl.when(jnp.logical_not(casing))
    def _():
        greet({"rad": rad + 1})

    @pl.when(jnp.logical_not(first))
    def _():
        each(lambda index: greet(device(sec - 1, index)))

    @pl.when(jnp.logical_not(last))
    def _():
        each(lambda index: greet(device(sec + 1, index)))

    @pl.when(first)
    def _():
        each(lambda index: greet(device(sec, index)), True)

    @pl.when(last)
    def _():
        each(lambda index: greet(device(sec, index)), True)

    blank = jnp.zeros((nr, lanes), jnp.float32)
    for v in range(nv):
        for slot in range(2):
            field[slot, rows(v * nx)] = blank
    for step in range(STEPS):
        for side in range(2):
            rad_out0[step, side] = blank

    @pl.when(floor)
    def _():
        for step in range(STEPS):
            rad_in[step, 0] = jnp.zeros(rad_in.shape[2:], jnp.float32)
            rad_in0[step, 0] = blank

    @pl.when(casing)
    def _():
        for step in range(STEPS):
            rad_in[step, 1] = jnp.zeros(rad_in.shape[2:], jnp.float32)
            rad_in0[step, 1] = blank

    def pressure_of(values):
        total = weight[0] * values[0]
        for v in range(1, nv):
            total = total + weight[v] * values[v]
        return total

    def pack_one(packs, value, index):
        to_left, to_right = packs
        to_left = jnp.where(lane == index, pltpu.roll(value, index, 1), to_left)
        to_right = jnp.where(lane == index, pltpu.roll(value, index + 1, 1), to_right)
        return to_left, to_right

    def pack_start(x, packs):
        for v in range(nv):
            packs = pack_one(packs, state[rows(v * nx + x)], v * nx + x)
        packs = pack_one(packs, viscosity[rows(x)], planes + x)
        return pack_one(packs, face_circum[rows(x)], planes + nx + x)

    for load in loads[:6]:
        load.wait()
    press_send[0] = pressure_of([state[rows(v * nx)] for v in range(nv)])
    press_send[STEPS] = pressure_of([outflow[rows(v)] for v in range(nv)])
    for v in range(nv):
        flow_send[0, rows(v)] = state[rows(v * nx + nx - 1)]
    for side, edge in ((0, 0), (1, nr - 1)):
        rad_out[0, side, pl.ds(0, planes)] = state[pl.ds(edge, planes, stride=nr)]
        rad_out[0, side, pl.ds(planes, nx)] = viscosity[pl.ds(edge, nx, stride=nr)]
        rad_out[0, side, pl.ds(planes + nx, nx)] = face_radial[pl.ds(edge, nx, stride=nr)]
    packs = lax.fori_loop(0, nx, pack_start, (blank, blank), unroll=True)
    row_out[0, 0, 0] = packs[0]
    row_out[0, 0, 1] = packs[1]

    one = jnp.int32(1)
    zero = jnp.int32(0)
    inner = group + group - jnp.where(jnp.logical_or(first, last), one, zero)
    inner = inner - (1 if n_sec == 1 else 0)
    beside = jnp.where(floor, zero, one) + jnp.where(casing, zero, one)
    pl.semaphore_wait(barrier, 2 + inner + beside)

    def send_flow(step):
        @pl.when(jnp.logical_not(last))
        def _():
            each(
                lambda index: send(
                    flow_send.at[step],
                    flow[step].at[mine],
                    flow_ss.at[step],
                    flow_rs.at[step],
                    device(sec + 1, index),
                )
            )

    def send_press(step):
        @pl.when(jnp.logical_not(first))
        def _():
            each(
                lambda index: send(
                    press_send.at[step],
                    press[step].at[mine],
                    press_ss.at[step],
                    press_rs.at[step],
                    device(sec - 1, index),
                )
            )

    def send_rows(step, part):
        for side, to in ((0, left), (1, right)):
            send(
                row_out.at[step, part, side],
                row_in.at[step, part, 1 - side],
                row_ss.at[step, part, side],
                row_rs.at[step, part, 1 - side],
                {"row": to},
            )

    def rad_refs(step, part, side):
        if part:
            return rad_out0.at[step, side], rad_in0.at[step, 1 - side]
        count = planes if step else planes + 2 * nx
        return (
            rad_out.at[step, side, pl.ds(0, count)],
            rad_in.at[step, 1 - side, pl.ds(0, count)],
        )

    def send_rads(step, part):
        for side, edge, to in ((0, floor, rad - 1), (1, casing, rad + 1)):

            @pl.when(jnp.logical_not(edge))
            def _(side=side, to=to):
                src, dst = rad_refs(step, part, side)
                send(
                    src,
                    dst,
                    rad_ss.at[step, part, side],
                    rad_rs.at[step, part, 1 - side],
                    {"rad": to},
                )

    def wait_beside(step, part):
        for side, edge in ((0, floor), (1, casing)):
            wait(row_in.at[step, part, side], row_rs.at[step, part, side])

            @pl.when(jnp.logical_not(edge))
            def _(side=side):
                wait(rad_refs(step, part, 1 - side)[1], rad_rs.at[step, part, side])

    send_rows(0, 0)
    send_rads(0, 0)
    send_press(0)

    @pl.when(last)
    def _():
        each(
            lambda index: send(
                press_send.at[STEPS],
                press[0].at[mine],
                edge_ss.at[1],
                press_rs.at[0],
                device(sec, index),
            ),
            True,
        )
        pltpu.make_async_copy(press_send.at[STEPS], press[0].at[mine], press_rs.at[0]).start()

    @pl.when(first)
    def _():
        each(
            lambda index: send(
                inflow, flow[0].at[mine], edge_ss.at[0], flow_rs.at[0], device(sec, index)
            ),
            True,
        )
        pltpu.make_async_copy(inflow, flow[0].at[mine], flow_rs.at[0]).start()

    send_flow(0)

    def lower_lane(value, packed, index):
        return jnp.where(
            lane == 0, pltpu.roll(packed, lax.rem(lanes - index, lanes), 1), pltpu.roll(value, 1, 1)
        )

    def upper_lane(value, packed, index):
        return jnp.where(
            lane == lanes - 1,
            pltpu.roll(packed, lanes - 1 - index, 1),
            pltpu.roll(value, lanes - 1, 1),
        )

    def lower_sub(value, edge_row):
        return jnp.where(sub == 0, edge_row, pltpu.roll(value, 1, 0))

    def upper_sub(value, edge_row):
        return jnp.where(sub == nr - 1, edge_row, pltpu.roll(value, nr - 1, 0))

    wall = jnp.logical_and(casing, sub == nr - 1)

    def put_direction(x, d, half, mu, lower, upper):
        area_l, mu_l = lower
        area_u, mu_u = upper
        mix_l, mix_u = half * area_l, half * area_u
        spread_l, spread_u = mix_l * (mu_l + mu), mix_u * (mu_u + mu)
        coef[5 * d, rows(x)] = mix_u
        coef[5 * d + 1, rows(x)] = mix_u - mix_l
        coef[5 * d + 2, rows(x)] = mix_l
        coef[5 * d + 3, rows(x)] = spread_u
        coef[5 * d + 4, rows(x)] = spread_l
        return spread_l + spread_u

    def prepare_axial(x, carry):
        below, above = jnp.maximum(x - 1, 0), jnp.minimum(x + 1, nx - 1)
        half = (0.5 * time_step) / volume[rows(x)]
        lower = face_axial[rows(below)], viscosity[rows(below)]
        upper = face_axial[rows(x)], viscosity[rows(above)]
        leaves = put_direction(x, 0, half, viscosity[rows(x)], lower, upper)
        coef[N_COEF - 1, rows(x)] = 1.0 - leaves
        coef[N_COEF, rows(x)] = half
        return carry

    def prepare_beside(x, carry):
        half = coef[N_COEF, rows(x)]
        mu = viscosity[rows(x)]
        area = jnp.where(wall, 0.0, face_radial[rows(x)])
        around = face_circum[rows(x)]
        from_left, from_right = row_in[0, 0, 0], row_in[0, 0, 1]
        lower = (
            lower_sub(area, rad_in[0, 0, pl.ds(planes + nx + x, 1)]),
            lower_sub(mu, rad_in[0, 0, pl.ds(planes + x, 1)]),
        )
        upper = area, upper_sub(mu, rad_in[0, 1, pl.ds(planes + x, 1)])
        leaves = put_direction(x, 1, half, mu, lower, upper)
        lower = (
            lower_lane(around, from_left, planes + nx + x),
            lower_lane(mu, from_left, planes + x),
        )
        upper = around, upper_lane(mu, from_right, planes + x)
        leaves = leaves + put_direction(x, 2, half, mu, lower, upper)
        coef[N_COEF - 1, rows(x)] = coef[N_COEF - 1, rows(x)] - leaves
        return carry

    for load in loads[6:]:
        load.wait()
    lax.fori_loop(0, nx, prepare_axial, 0, unroll=True)
    wait_beside(0, 0)
    prepare_beside(nx - 1, 0)

    def advance(x, centre, before, after, packed, edge_rows):
        from_left, from_right = packed
        c = [coef[k, rows(x)] for k in range(N_COEF)]
        mixed, fresh = [], []
        for v in range(nv):
            index = v * nx + x
            mid = centre[v]
            below, above = edge_rows(v)
            pairs = (
                (before[v], after[v]),
                (lower_sub(mid, below), upper_sub(mid, above)),
                (lower_lane(mid, from_left, index), upper_lane(mid, from_right, index)),
            )
            kept = c[N_COEF - 1] * mid
            for d, (lo, hi) in enumerate(pairs):
                mixed.append(c[5 * d] * hi + c[5 * d + 1] * mid - c[5 * d + 2] * lo)
                kept = kept + (c[5 * d + 3] * hi + c[5 * d + 4] * lo)
            fresh.append(kept)
        result = []
        for u in range(nv):
            total = None
            for d in range(3):
                for v in range(nv):
                    term = matrix[d * nv + u, 0, v] * mixed[3 * v + d]
                    total = term if total is None else total + term
            result.append(fresh[u] - total)
        return result

    for step in range(STEPS):
        final = step == STEPS - 1
        src = state if step == 0 else field.at[(step - 1) % 2]
        dst = out if final else field.at[step % 2]
        if step:
            wait_beside(step, 0)

        def plane(x):
            return [src[rows(v * nx + x)] for v in range(nv)]

        def keep_plane(x, values):
            for v in range(nv):
                dst[rows(v * nx + x)] = values[v]

        def pack_plane(x, values, packs):
            if final:
                return packs
            for v in range(nv):
                packs = pack_one(packs, values[v], v * nx + x)
            return packs

        def edge_rows_at(x, step=step):
            def edge_rows(v):
                at = pl.ds(v * nx + x, 1)
                return rad_in[step, 0, at], rad_in[step, 1, at]

            return edge_rows

        def inside(x, packs):
            packed = row_in[step, 0, 0], row_in[step, 0, 1]
            values = advance(
                x, plane(x), plane(x - 1), plane(x + 1), packed, edge_rows_at(x)
            )
            keep_plane(x, values)
            return pack_plane(x, values, packs)

        def all_inside(packs):
            return lax.fori_loop(1, nx - 1, inside, packs, unroll=True)

        packs = blank, blank
        if step:
            packs = all_inside(packs)

        def take_press(step=step):
            wait(press[step], press_rs.at[step])
            for a in range(nr):
                donor = up[0, a]
                at = pl.ds(lax.rem(donor, nr), 1)
                mapped[pl.ds(a, 1)] = press[step][lax.div(donor, nr), at]

        if step:
            pl.when(jnp.logical_not(last))(take_press)
        else:
            take_press()
        centre = plane(nx - 1)
        gap = mapped[...] - pressure_of(centre)
        after = [centre[v] + coupling[v] * gap for v in range(nv)]
        packed = row_in[step, 0, 0], row_in[step, 0, 1]
        values = advance(
            nx - 1, centre, plane(nx - 2), after, packed, edge_rows_at(nx - 1)
        )
        keep_plane(nx - 1, values)
        if not final:
            for v in range(nv):
                flow_send[step + 1, rows(v)] = values[v]
            send_flow(step + 1)
        if step == 0:
            lax.fori_loop(0, nx - 1, prepare_beside, 0, unroll=True)
            packs = all_inside(packs)
        if not final:
            packs = pack_plane(nx - 1, values, packs)
            row_out[step + 1, 0, 0] = packs[0]
            row_out[step + 1, 0, 1] = packs[1]
            send_rows(step + 1, 0)
            for side, edge in ((0, 0), (1, nr - 1)):
                rad_out[step + 1, side, pl.ds(0, planes)] = dst[pl.ds(edge, planes, stride=nr)]
            send_rads(step + 1, 0)

        def take_flow(step=step):
            wait(flow[step], flow_rs.at[step])
            for a in range(nr):
                donor = down[0, a]
                owner, base = lax.div(donor, nr), lax.rem(donor, nr)
                for v in range(nv):
                    ghost[pl.ds(v * nr + a, 1)] = flow[step][owner, pl.ds(v * nr + base, 1)]

        if step:
            wait_beside(step, 1)
            pl.when(jnp.logical_not(first))(take_flow)

            def edge_rows(v, step=step):
                at = pl.ds(v, 1)
                return rad_in0[step, 0, at], rad_in0[step, 1, at]

            packed = row_in[step, 1, 0], row_in[step, 1, 1]
        else:
            take_flow()
            edge_rows = edge_rows_at(0)
        before = [ghost[rows(v)] for v in range(nv)]
        values = advance(0, plane(0), before, plane(1), packed, edge_rows)
        keep_plane(0, values)
        if not final:
            press_send[step + 1] = pressure_of(values)
            send_press(step + 1)
            packs = pack_plane(0, values, (blank, blank))
            row_out[step + 1, 1, 0] = packs[0]
            row_out[step + 1, 1, 1] = packs[1]
            send_rows(step + 1, 1)
            for v in range(nv):
                rad_out0[step + 1, 0, pl.ds(v, 1)] = values[v][:1]
                rad_out0[step + 1, 1, pl.ds(v, 1)] = values[v][nr - 1 :]
            send_rads(step + 1, 1)

    for step in range(STEPS):
        for part in range(2 if step else 1):
            for side, edge in ((0, floor), (1, casing)):
                wait(row_out.at[step, part, side], row_ss.at[step, part, side])

                @pl.when(jnp.logical_not(edge))
                def _(step=step, part=part, side=side):
                    wait(rad_refs(step, part, side)[0], rad_ss.at[step, part, side])

    @pl.when(jnp.logical_not(last))
    def _():
        for step in range(STEPS):
            wait(flow[step], flow_ss.at[step])

    @pl.when(jnp.logical_not(first))
    def _():
        for step in range(STEPS):
            wait(press[step], press_ss.at[step])

    @pl.when(first)
    def _():
        wait(flow[0].at[pl.ds(0, group - 1)], edge_ss.at[0])

    @pl.when(last)
    def _():
        wait(press[0].at[pl.ds(0, group - 1)], edge_ss.at[1])


def body(
    n_sec,
    n_row,
    n_rad,
    state,
    volume,
    face_axial,
    face_radial,
    face_circum,
    viscosity,
    flux_matrix,
    inflow_plane,
    outflow_plane,
    down_donors,
    up_donors,
    pressure_weight,
    boundary_coupling,
):
    nv, _, nx, nr, lanes = state.shape
    group = n_row * n_rad
    planes, block = nv * nx, nv * nr
    held = planes + 2 * nx

    def flat(array):
        return array.reshape(-1, lanes)

    def vmem(*shape):
        return pltpu.VMEM(shape, jnp.float32)

    dma = pltpu.SemaphoreType.DMA
    in_vmem = pl.BlockSpec(memory_space=pltpu.VMEM)
    result = pl.pallas_call(
        functools.partial(kernel, (n_sec, n_row, n_rad, nv, nx, nr, lanes)),
        out_shape=pltpu.VMEM((planes * nr, lanes), jnp.float32),
        in_specs=[pl.BlockSpec(memory_space=pltpu.HBM)] * 13,
        out_specs=in_vmem,
        scratch_shapes=[
            vmem(planes * nr, lanes),
            *[vmem(nx * nr, lanes)] * 5,
            pltpu.SMEM((3 * nv, 1, nv), jnp.float32),
            vmem(block, lanes),
            pltpu.SMEM(down_donors.shape, jnp.int32),
            pltpu.SMEM(up_donors.shape, jnp.int32),
            pltpu.SMEM(pressure_weight.shape, jnp.float32),
            pltpu.SMEM(boundary_coupling.shape, jnp.float32),
            dma((12,)),
            vmem(2, planes * nr, lanes),
            vmem(N_COEF + 1, nx * nr, lanes),
            [vmem(group, block, lanes)] * STEPS,
            vmem(STEPS, block, lanes),
            [vmem(group, nr, lanes)] * STEPS,
            vmem(STEPS + 1, nr, lanes),
            vmem(block, lanes),
            vmem(nr, lanes),
            vmem(STEPS, 2, 2, nr, lanes),
            vmem(STEPS, 2, 2, nr, lanes),
            vmem(STEPS, 2, held, lanes),
            vmem(STEPS, 2, held, lanes),
            vmem(STEPS, 2, nr, lanes),
            vmem(STEPS, 2, nr, lanes),
            dma((STEPS,)),
            dma((STEPS,)),
            dma((STEPS,)),
            dma((STEPS,)),
            dma((2,)),
            dma((STEPS, 2, 2)),
            dma((STEPS, 2, 2)),
            dma((STEPS, 2, 2)),
            dma((STEPS, 2, 2)),
        ],
        compiler_params=pltpu.CompilerParams(
            collective_id=0, has_side_effects=True, vmem_limit_bytes=60 * 1024 * 1024
        ),
        name="coupled_steps",
    )(
        flat(state),
        flat(volume),
        flat(face_axial),
        flat(face_radial),
        flat(face_circum),
        flat(viscosity),
        flux_matrix.transpose(1, 2, 0, 3).reshape(3 * nv, 1, nv),
        flat(inflow_plane),
        flat(outflow_plane),
        down_donors,
        up_donors,
        pressure_weight,
        boundary_coupling,
    )
    return result.reshape(state.shape)


def solution(mesh):
    in_specs = (
        P(None, "sec", None, "rad", "row"),
        P("sec", None, "rad", "row"),
        P("sec", None, "rad", "row"),
        P("sec", None, "rad", "row"),
        P("sec", None, "rad", "row"),
        P("sec", None, "rad", "row"),
        P("sec", None, None, None),
        P(None, "rad", "row"),
        P(None, "rad", "row"),
        P("sec", ("row", "rad")),
        P("sec", ("row", "rad")),
        P(),
        P(),
    )
    out_specs = P(None, "sec", None, "rad", "row")
    sizes = tuple(mesh.shape[name] for name in ("sec", "row", "rad"))
    return jax.shard_map(
        functools.partial(body, *sizes),
        mesh=mesh,
        in_specs=in_specs,
        out_specs=out_specs,
        check_vma=False,
    )
```

```python
import functools

import jax
import jax.numpy as jnp
from jax import lax
from jax.experimental import pallas as pl
from jax.experimental.pallas import tpu as pltpu
from jax.sharding import PartitionSpec as P

STEPS = 4


time_step = 0.08

MESH = pl.DeviceIdType.MESH
N_COEF = 16


def kernel(
    sizes,
    state_hbm,
    volume_hbm,
    face_axial_hbm,
    face_radial_hbm,
    face_circum_hbm,
    viscosity_hbm,
    matrix_hbm,
    inflow,
    outflow_hbm,
    down_hbm,
    up_hbm,
    weight_hbm,
    coupling_hbm,
    out,
    state,
    volume,
    face_axial,
    face_radial,
    face_circum,
    viscosity,
    matrix,
    outflow,
    down,
    up,
    weight,
    coupling,
    loaded,
    field,
    coef,
    flow,
    flow_send,
    press,
    press_send,
    ghost,
    mapped,
    base,
    row_in,
    row_out,
    rad_in,
    rad_out,
    rad_in0,
    rad_out0,
    flow_ss,
    flow_rs,
    pass_ss,
    pass_rs,
    press_ss,
    press_rs,
    edge_ss,
    row_ss,
    row_rs,
    rad_ss,
    rad_rs,
):
    n_sec, n_row, n_rad, nv, nx, nr, lanes = sizes
    group = n_row * n_rad
    planes = nv * nx
    sec, row, rad = lax.axis_index("sec"), lax.axis_index("row"), lax.axis_index("rad")
    mine = row * n_rad + rad
    first, last = sec == 0, sec == n_sec - 1
    floor, casing = rad == 0, rad == n_rad - 1
    right, left = lax.rem(row + 1, n_row), lax.rem(row + n_row - 1, n_row)
    lane = lax.broadcasted_iota(jnp.int32, (nr, lanes), 1)
    sub = lax.broadcasted_iota(jnp.int32, (nr, lanes), 0)

    def device(section, index):
        return {"sec": section, "row": lax.div(index, n_rad), "rad": lax.rem(index, n_rad)}

    def each(action, skip_self=False):
        def one(i):
            index = lax.rem(mine + i, group)
            action(index)

        start = 1 if skip_self else 0
        if group <= 16:
            for i in range(start, group):
                one(i)
        else:
            pl.loop(start, group)(one)

    half_group = group // 2
    parity = lax.rem(row, 2)
    pair = row + 1 - 2 * parity
    spot = lax.div(row, 2) * n_rad + rad

    def alike(index):
        return {
            "row": 2 * lax.div(index, n_rad) + parity,
            "rad": lax.rem(index, n_rad),
        }

    def each_alike(action, skip_self=False):
        def one(i):
            action(alike(lax.rem(spot + i, half_group)))

        start = 1 if skip_self else 0
        if group <= 16:
            for i in range(start, half_group):
                one(i)
        else:
            pl.loop(start, half_group)(one)

    def slot_of(owner):
        across, along = lax.div(owner, n_rad), lax.rem(owner, n_rad)
        return lax.rem(across, 2) * half_group + lax.div(across, 2) * n_rad + along

    def send(src, dst, send_sem, recv_sem, to):
        pltpu.make_async_remote_copy(
            src_ref=src,
            dst_ref=dst,
            send_sem=send_sem,
            recv_sem=recv_sem,
            device_id=to,
            device_id_type=MESH,
        ).start()

    def wait(ref, sem):
        pltpu.make_async_copy(ref, ref, sem).wait()

    def rows(index):
        if isinstance(index, int):
            return pl.ds(index * nr, nr)
        return pl.ds(pl.multiple_of(index * nr, nr), nr)

    loads = [
        pltpu.make_async_copy(src, dst, loaded.at[i])
        for i, (src, dst) in enumerate(
            (
                (state_hbm, state),
                (viscosity_hbm, viscosity),
                (face_circum_hbm, face_circum),
                (face_radial_hbm, face_radial),
                (weight_hbm, weight),
                (outflow_hbm, outflow),
                (volume_hbm, volume),
                (face_axial_hbm, face_axial),
                (up_hbm, up),
                (coupling_hbm, coupling),
                (matrix_hbm, matrix),
                (down_hbm, down),
            )
        )
    ]
    for load in loads:
        load.start()

    barrier = pltpu.get_barrier_semaphore()

    def greet(to):
        pl.semaphore_signal(barrier, inc=1, device_id=to, device_id_type=MESH)

    greet({"row": left})
    greet({"row": right})

    @pl.when(jnp.logical_not(floor))
    def _():
        greet({"rad": rad - 1})

    @pl.when(jnp.logical_not(casing))
    def _():
        greet({"rad": rad + 1})

    @pl.when(jnp.logical_not(first))
    def _():
        each(lambda index: greet(device(sec - 1, index)))

    @pl.when(jnp.logical_not(last))
    def _():
        each(lambda index: greet(device(sec + 1, index)))

    @pl.when(first)
    def _():
        each(lambda index: greet(device(sec, index)), True)

    @pl.when(last)
    def _():
        each(lambda index: greet(device(sec, index)), True)

    blank = jnp.zeros((nr, lanes), jnp.float32)
    for v in range(nv):
        for slot in range(2):
            field[slot, rows(v * nx)] = blank
    for step in range(STEPS):
        for side in range(2):
            rad_out0[step, side] = blank

    @pl.when(floor)
    def _():
        for step in range(STEPS):
            rad_in[step, 0] = jnp.zeros(rad_in.shape[2:], jnp.float32)
            rad_in0[step, 0] = blank

    @pl.when(casing)
    def _():
        for step in range(STEPS):
            rad_in[step, 1] = jnp.zeros(rad_in.shape[2:], jnp.float32)
            rad_in0[step, 1] = blank

    def pressure_of(values):
        total = weight[0] * values[0]
        for v in range(1, nv):
            total = total + weight[v] * values[v]
        return total

    def pack_one(packs, value, index):
        to_left, to_right = packs
        to_left = jnp.where(lane == index, pltpu.roll(value, index, 1), to_left)
        to_right = jnp.where(lane == index, pltpu.roll(value, index + 1, 1), to_right)
        return to_left, to_right

    def pack_start(x, packs):
        for v in range(nv):
            packs = pack_one(packs, state[rows(v * nx + x)], v * nx + x)
        packs = pack_one(packs, viscosity[rows(x)], planes + x)
        return pack_one(packs, face_circum[rows(x)], planes + nx + x)

    for load in loads[:6]:
        load.wait()
    press_send[0] = pressure_of([state[rows(v * nx)] for v in range(nv)])
    press_send[STEPS] = pressure_of([outflow[rows(v)] for v in range(nv)])
    for v in range(nv):
        flow_send[0, rows(v)] = state[rows(v * nx + nx - 1)]
    for side, edge in ((0, 0), (1, nr - 1)):
        rad_out[0, side, pl.ds(0, planes)] = state[pl.ds(edge, planes, stride=nr)]
        rad_out[0, side, pl.ds(planes, nx)] = viscosity[pl.ds(edge, nx, stride=nr)]
        rad_out[0, side, pl.ds(planes + nx, nx)] = face_radial[pl.ds(edge, nx, stride=nr)]
    packs = lax.fori_loop(0, nx, pack_start, (blank, blank), unroll=True)
    row_out[0, 0, 0] = packs[0]
    row_out[0, 0, 1] = packs[1]

    one = jnp.int32(1)
    zero = jnp.int32(0)
    inner = group + group - jnp.where(jnp.logical_or(first, last), one, zero)
    inner = inner - (1 if n_sec == 1 else 0)
    beside = jnp.where(floor, zero, one) + jnp.where(casing, zero, one)
    pl.semaphore_wait(barrier, 2 + inner + beside)

    def send_flow(step):
        @pl.when(jnp.logical_not(last))
        def _():
            each_alike(
                lambda to: send(
                    flow_send.at[step],
                    flow[step].at[parity * half_group + spot],
                    flow_ss.at[step],
                    flow_rs.at[step],
                    {"sec": sec + 1, **to},
                )
            )

    def halves(step):
        own = flow[step].at[pl.ds(parity * half_group, half_group)]
        other = flow[step].at[pl.ds((1 - parity) * half_group, half_group)]
        return own, other

    def pass_flow(step):
        def go():
            own, _ = halves(step)
            wait(own, flow_rs.at[step])
            send(own, own, pass_ss.at[step], pass_rs.at[step], {"row": pair})

        if step:
            pl.when(jnp.logical_not(first))(go)
        else:
            go()

    def send_press(step):
        @pl.when(jnp.logical_not(first))
        def _():
            each(
                lambda index: send(
                    press_send.at[step],
                    press[step].at[mine],
                    press_ss.at[step],
                    press_rs.at[step],
                    device(sec - 1, index),
                )
            )

    def send_rows(step, part):
        for side, to in ((0, left), (1, right)):
            send(
                row_out.at[step, part, side],
                row_in.at[step, part, 1 - side],
                row_ss.at[step, part, side],
                row_rs.at[step, part, 1 - side],
                {"row": to},
            )

    def rad_refs(step, part, side):
        if part:
            return rad_out0.at[step, side], rad_in0.at[step, 1 - side]
        count = planes if step else planes + 2 * nx
        return (
            rad_out.at[step, side, pl.ds(0, count)],
            rad_in.at[step, 1 - side, pl.ds(0, count)],
        )

    def send_rads(step, part):
        for side, edge, to in ((0, floor, rad - 1), (1, casing, rad + 1)):

            @pl.when(jnp.logical_not(edge))
            def _(side=side, to=to):
                src, dst = rad_refs(step, part, side)
                send(
                    src,
                    dst,
                    rad_ss.at[step, part, side],
                    rad_rs.at[step, part, 1 - side],
                    {"rad": to},
                )

    def wait_beside(step, part):
        for side, edge in ((0, floor), (1, casing)):
            wait(row_in.at[step, part, side], row_rs.at[step, part, side])

            @pl.when(jnp.logical_not(edge))
            def _(side=side):
                wait(rad_refs(step, part, 1 - side)[1], rad_rs.at[step, part, side])

    send_rows(0, 0)
    send_rads(0, 0)
    send_press(0)

    @pl.when(last)
    def _():
        each(
            lambda index: send(
                press_send.at[STEPS],
                press[0].at[mine],
                edge_ss.at[1],
                press_rs.at[0],
                device(sec, index),
            ),
            True,
        )
        pltpu.make_async_copy(press_send.at[STEPS], press[0].at[mine], press_rs.at[0]).start()

    @pl.when(first)
    def _():
        place = flow[0].at[parity * half_group + spot]
        each_alike(
            lambda to: send(inflow, place, edge_ss.at[0], flow_rs.at[0], to), True
        )
        pltpu.make_async_copy(inflow, place, flow_rs.at[0]).start()

    send_flow(0)

    def lower_lane(value, packed, index):
        return jnp.where(
            lane == 0, pltpu.roll(packed, lax.rem(lanes - index, lanes), 1), pltpu.roll(value, 1, 1)
        )

    def upper_lane(value, packed, index):
        return jnp.where(
            lane == lanes - 1,
            pltpu.roll(packed, lanes - 1 - index, 1),
            pltpu.roll(value, lanes - 1, 1),
        )

    def lower_sub(value, edge_row):
        return jnp.where(sub == 0, edge_row, pltpu.roll(value, 1, 0))

    def upper_sub(value, edge_row):
        return jnp.where(sub == nr - 1, edge_row, pltpu.roll(value, nr - 1, 0))

    wall = jnp.logical_and(casing, sub == nr - 1)

    def put_direction(x, d, half, mu, lower, upper):
        area_l, mu_l = lower
        area_u, mu_u = upper
        mix_l, mix_u = half * area_l, half * area_u
        spread_l, spread_u = mix_l * (mu_l + mu), mix_u * (mu_u + mu)
        coef[5 * d, rows(x)] = mix_u
        coef[5 * d + 1, rows(x)] = mix_u - mix_l
        coef[5 * d + 2, rows(x)] = mix_l
        coef[5 * d + 3, rows(x)] = spread_u
        coef[5 * d + 4, rows(x)] = spread_l
        return spread_l + spread_u

    def prepare_axial(x, carry):
        below, above = jnp.maximum(x - 1, 0), jnp.minimum(x + 1, nx - 1)
        half = (0.5 * time_step) / volume[rows(x)]
        lower = face_axial[rows(below)], viscosity[rows(below)]
        upper = face_axial[rows(x)], viscosity[rows(above)]
        leaves = put_direction(x, 0, half, viscosity[rows(x)], lower, upper)
        coef[N_COEF - 1, rows(x)] = 1.0 - leaves
        coef[N_COEF, rows(x)] = half
        return carry

    def prepare_beside(x, carry):
        half = coef[N_COEF, rows(x)]
        mu = viscosity[rows(x)]
        area = jnp.where(wall, 0.0, face_radial[rows(x)])
        around = face_circum[rows(x)]
        from_left, from_right = row_in[0, 0, 0], row_in[0, 0, 1]
        lower = (
            lower_sub(area, rad_in[0, 0, pl.ds(planes + nx + x, 1)]),
            lower_sub(mu, rad_in[0, 0, pl.ds(planes + x, 1)]),
        )
        upper = area, upper_sub(mu, rad_in[0, 1, pl.ds(planes + x, 1)])
        leaves = put_direction(x, 1, half, mu, lower, upper)
        lower = (
            lower_lane(around, from_left, planes + nx + x),
            lower_lane(mu, from_left, planes + x),
        )
        upper = around, upper_lane(mu, from_right, planes + x)
        leaves = leaves + put_direction(x, 2, half, mu, lower, upper)
        coef[N_COEF - 1, rows(x)] = coef[N_COEF - 1, rows(x)] - leaves
        return carry

    for load in loads[6:]:
        load.wait()
    lax.fori_loop(0, nx, prepare_axial, 0, unroll=True)
    wait_beside(0, 0)
    prepare_beside(nx - 1, 0)

    def advance(x, centre, before, after, packed, edge_rows):
        from_left, from_right = packed
        c = [coef[k, rows(x)] for k in range(N_COEF)]
        mixed, fresh = [], []
        for v in range(nv):
            index = v * nx + x
            mid = centre[v]
            below, above = edge_rows(v)
            pairs = (
                (before and before[v], after and after[v]),
                (lower_sub(mid, below), upper_sub(mid, above)),
                (lower_lane(mid, from_left, index), upper_lane(mid, from_right, index)),
            )
            kept = c[N_COEF - 1] * mid
            for d, (lo, hi) in enumerate(pairs):
                mix = c[5 * d + 1] * mid
                if hi is not None:
                    mix = mix + c[5 * d] * hi
                    kept = kept + c[5 * d + 3] * hi
                if lo is not None:
                    mix = mix - c[5 * d + 2] * lo
                    kept = kept + c[5 * d + 4] * lo
                mixed.append(mix)
            fresh.append(kept)
        result = []
        for u in range(nv):
            total = None
            for d in range(3):
                for v in range(nv):
                    term = matrix[d * nv + u, 0, v] * mixed[3 * v + d]
                    total = term if total is None else total + term
            result.append(fresh[u] - total)
        return result

    def complete(x, ghosts, mix_at, keep_at):
        mix, spread = coef[mix_at, rows(x)], coef[keep_at, rows(x)]
        mixed = [mix * ghosts[v] for v in range(nv)]
        result = []
        for u in range(nv):
            total = matrix[u, 0, 0] * mixed[0]
            for v in range(1, nv):
                total = total + matrix[u, 0, v] * mixed[v]
            if mix_at == 0:
                total = -total
            result.append((base[rows(u)] + spread * ghosts[u]) + total)
        return result

    def keep_base(values):
        for v in range(nv):
            base[rows(v)] = values[v]

    for step in range(STEPS):
        final = step == STEPS - 1
        src = state if step == 0 else field.at[(step - 1) % 2]
        dst = out if final else field.at[step % 2]
        if step:
            wait_beside(step, 0)

        def plane(x):
            return [src[rows(v * nx + x)] for v in range(nv)]

        def keep_plane(x, values):
            for v in range(nv):
                dst[rows(v * nx + x)] = values[v]

        def pack_plane(x, values, packs):
            if final:
                return packs
            for v in range(nv):
                packs = pack_one(packs, values[v], v * nx + x)
            return packs

        def edge_rows_at(x, step=step):
            def edge_rows(v):
                at = pl.ds(v * nx + x, 1)
                return rad_in[step, 0, at], rad_in[step, 1, at]

            return edge_rows

        def inside(x, packs):
            packed = row_in[step, 0, 0], row_in[step, 0, 1]
            values = advance(
                x, plane(x), plane(x - 1), plane(x + 1), packed, edge_rows_at(x)
            )
            keep_plane(x, values)
            return pack_plane(x, values, packs)

        def all_inside(packs):
            return lax.fori_loop(1, nx - 1, inside, packs, unroll=True)

        packs = blank, blank
        if step:
            packs = all_inside(packs)

        centre = plane(nx - 1)
        packed = row_in[step, 0, 0], row_in[step, 0, 1]
        keep_base(
            advance(nx - 1, centre, plane(nx - 2), None, packed, edge_rows_at(nx - 1))
        )
        if step:
            pass_flow(step)

        def take_press(step=step):
            donors = [up[0, a] for a in range(nr)]
            spots = [(lax.div(donor, nr), lax.rem(donor, nr)) for donor in donors]
            wait(press[step], press_rs.at[step])
            for a, (owner, at) in enumerate(spots):
                mapped[pl.ds(a, 1)] = press[step][owner, pl.ds(at, 1)]

        if step:
            pl.when(jnp.logical_not(last))(take_press)
        else:
            take_press()
        centre = plane(nx - 1)
        gap = mapped[...] - pressure_of(centre)
        after = [centre[v] + coupling[v] * gap for v in range(nv)]
        values = complete(nx - 1, after, 0, 3)
        keep_plane(nx - 1, values)
        if not final:
            for v in range(nv):
                flow_send[step + 1, rows(v)] = values[v]
            send_flow(step + 1)
        if step == 0:
            pass_flow(0)
            lax.fori_loop(0, nx - 1, prepare_beside, 0, unroll=True)
            packs = all_inside(packs)
        if not final:
            packs = pack_plane(nx - 1, values, packs)
            row_out[step + 1, 0, 0] = packs[0]
            row_out[step + 1, 0, 1] = packs[1]
            send_rows(step + 1, 0)
            for side, edge in ((0, 0), (1, nr - 1)):
                rad_out[step + 1, side, pl.ds(0, planes)] = dst[pl.ds(edge, planes, stride=nr)]
            send_rads(step + 1, 0)

        def take_flow(step=step):
            donors = [down[0, a] for a in range(nr)]
            spots = [
                (slot_of(lax.div(donor, nr)), lax.rem(donor, nr)) for donor in donors
            ]
            wait(halves(step)[1], pass_rs.at[step])
            for a, (owner, at) in enumerate(spots):
                for v in range(nv):
                    ghost[pl.ds(v * nr + a, 1)] = flow[step][owner, pl.ds(v * nr + at, 1)]

        if step:
            wait_beside(step, 1)

            def edge_rows(v, step=step):
                at = pl.ds(v, 1)
                return rad_in0[step, 0, at], rad_in0[step, 1, at]

            packed = row_in[step, 1, 0], row_in[step, 1, 1]
        else:
            edge_rows = edge_rows_at(0)
        keep_base(advance(0, plane(0), None, plane(1), packed, edge_rows))
        if step:
            pl.when(jnp.logical_not(first))(take_flow)
        else:
            take_flow()
        values = complete(0, [ghost[rows(v)] for v in range(nv)], 2, 4)
        keep_plane(0, values)
        if not final:
            press_send[step + 1] = pressure_of(values)
            send_press(step + 1)
            packs = pack_plane(0, values, (blank, blank))
            row_out[step + 1, 1, 0] = packs[0]
            row_out[step + 1, 1, 1] = packs[1]
            send_rows(step + 1, 1)
            for v in range(nv):
                rad_out0[step + 1, 0, pl.ds(v, 1)] = values[v][:1]
                rad_out0[step + 1, 1, pl.ds(v, 1)] = values[v][nr - 1 :]
            send_rads(step + 1, 1)

    wait(halves(0)[0], pass_ss.at[0])

    @pl.when(jnp.logical_not(first))
    def _():
        for step in range(1, STEPS):
            wait(halves(step)[0], pass_ss.at[step])

    for step in range(STEPS):
        for part in range(2 if step else 1):
            for side, edge in ((0, floor), (1, casing)):
                wait(row_out.at[step, part, side], row_ss.at[step, part, side])

                @pl.when(jnp.logical_not(edge))
                def _(step=step, part=part, side=side):
                    wait(rad_refs(step, part, side)[0], rad_ss.at[step, part, side])

    @pl.when(jnp.logical_not(last))
    def _():
        for step in range(STEPS):
            wait(flow[step].at[pl.ds(0, half_group)], flow_ss.at[step])

    @pl.when(jnp.logical_not(first))
    def _():
        for step in range(STEPS):
            wait(press[step], press_ss.at[step])

    @pl.when(first)
    def _():
        wait(flow[0].at[pl.ds(0, half_group - 1)], edge_ss.at[0])

    @pl.when(last)
    def _():
        wait(press[0].at[pl.ds(0, group - 1)], edge_ss.at[1])


def body(
    n_sec,
    n_row,
    n_rad,
    state,
    volume,
    face_axial,
    face_radial,
    face_circum,
    viscosity,
    flux_matrix,
    inflow_plane,
    outflow_plane,
    down_donors,
    up_donors,
    pressure_weight,
    boundary_coupling,
):
    nv, _, nx, nr, lanes = state.shape
    group = n_row * n_rad
    planes, block = nv * nx, nv * nr
    held = planes + 2 * nx

    def flat(array):
        return array.reshape(-1, lanes)

    def vmem(*shape):
        return pltpu.VMEM(shape, jnp.float32)

    dma = pltpu.SemaphoreType.DMA
    in_vmem = pl.BlockSpec(memory_space=pltpu.VMEM)
    result = pl.pallas_call(
        functools.partial(kernel, (n_sec, n_row, n_rad, nv, nx, nr, lanes)),
        out_shape=pltpu.VMEM((planes * nr, lanes), jnp.float32),
        in_specs=[pl.BlockSpec(memory_space=pltpu.HBM)] * 13,
        out_specs=in_vmem,
        scratch_shapes=[
            vmem(planes * nr, lanes),
            *[vmem(nx * nr, lanes)] * 5,
            pltpu.SMEM((3 * nv, 1, nv), jnp.float32),
            vmem(block, lanes),
            pltpu.SMEM(down_donors.shape, jnp.int32),
            pltpu.SMEM(up_donors.shape, jnp.int32),
            pltpu.SMEM(pressure_weight.shape, jnp.float32),
            pltpu.SMEM(boundary_coupling.shape, jnp.float32),
            dma((12,)),
            vmem(2, planes * nr, lanes),
            vmem(N_COEF + 1, nx * nr, lanes),
            [vmem(group, block, lanes)] * STEPS,
            vmem(STEPS, block, lanes),
            [vmem(group, nr, lanes)] * STEPS,
            vmem(STEPS + 1, nr, lanes),
            vmem(block, lanes),
            vmem(nr, lanes),
            vmem(block, lanes),
            vmem(STEPS, 2, 2, nr, lanes),
            vmem(STEPS, 2, 2, nr, lanes),
            vmem(STEPS, 2, held, lanes),
            vmem(STEPS, 2, held, lanes),
            vmem(STEPS, 2, nr, lanes),
            vmem(STEPS, 2, nr, lanes),
            dma((STEPS,)),
            dma((STEPS,)),
            dma((STEPS,)),
            dma((STEPS,)),
            dma((STEPS,)),
            dma((STEPS,)),
            dma((2,)),
            dma((STEPS, 2, 2)),
            dma((STEPS, 2, 2)),
            dma((STEPS, 2, 2)),
            dma((STEPS, 2, 2)),
        ],
        compiler_params=pltpu.CompilerParams(
            collective_id=0, has_side_effects=True, vmem_limit_bytes=60 * 1024 * 1024
        ),
        name="coupled_steps",
    )(
        flat(state),
        flat(volume),
        flat(face_axial),
        flat(face_radial),
        flat(face_circum),
        flat(viscosity),
        flux_matrix.transpose(1, 2, 0, 3).reshape(3 * nv, 1, nv),
        flat(inflow_plane),
        flat(outflow_plane),
        down_donors,
        up_donors,
        pressure_weight,
        boundary_coupling,
    )
    return result.reshape(state.shape)


def solution(mesh):
    in_specs = (
        P(None, "sec", None, "rad", "row"),
        P("sec", None, "rad", "row"),
        P("sec", None, "rad", "row"),
        P("sec", None, "rad", "row"),
        P("sec", None, "rad", "row"),
        P("sec", None, "rad", "row"),
        P("sec", None, None, None),
        P(None, "rad", "row"),
        P(None, "rad", "row"),
        P("sec", ("row", "rad")),
        P("sec", ("row", "rad")),
        P(),
        P(),
    )
    out_specs = P(None, "sec", None, "rad", "row")
    sizes = tuple(mesh.shape[name] for name in ("sec", "row", "rad"))
    return jax.shard_map(
        functools.partial(body, *sizes),
        mesh=mesh,
        in_specs=in_specs,
        out_specs=out_specs,
        check_vma=False,
    )
```

```python
import functools

import jax
import jax.numpy as jnp
from jax import lax
from jax.experimental import pallas as pl
from jax.experimental.pallas import tpu as pltpu
from jax.sharding import PartitionSpec as P

STEPS = 4


time_step = 0.08

MESH = pl.DeviceIdType.MESH
N_COEF = 16


def kernel(
    sizes,
    state_hbm,
    volume_hbm,
    face_axial_hbm,
    face_radial_hbm,
    face_circum_hbm,
    viscosity_hbm,
    matrix_hbm,
    inflow,
    outflow_hbm,
    down_hbm,
    up_hbm,
    weight_hbm,
    coupling_hbm,
    out,
    state,
    volume,
    face_axial,
    face_radial,
    face_circum,
    viscosity,
    matrix,
    outflow,
    down,
    up,
    weight,
    coupling,
    loaded,
    field,
    coef,
    flow,
    flow_send,
    press,
    press_send,
    ghost,
    mapped,
    base,
    row_in,
    row_out,
    rad_in,
    rad_out,
    rad_in0,
    rad_out0,
    flow_ss,
    flow_rs,
    pass_ss,
    pass_rs,
    press_ss,
    press_rs,
    edge_ss,
    row_ss,
    row_rs,
    rad_ss,
    rad_rs,
):
    n_sec, n_row, n_rad, nv, nx, nr, lanes = sizes
    group = n_row * n_rad
    planes = nv * nx
    sec, row, rad = lax.axis_index("sec"), lax.axis_index("row"), lax.axis_index("rad")
    mine = row * n_rad + rad
    first, last = sec == 0, sec == n_sec - 1
    floor, casing = rad == 0, rad == n_rad - 1
    right, left = lax.rem(row + 1, n_row), lax.rem(row + n_row - 1, n_row)
    lane = lax.broadcasted_iota(jnp.int32, (nr, lanes), 1)
    sub = lax.broadcasted_iota(jnp.int32, (nr, lanes), 0)

    def device(section, index):
        return {"sec": section, "row": lax.div(index, n_rad), "rad": lax.rem(index, n_rad)}

    def each(action, skip_self=False):
        def one(i):
            index = lax.rem(mine + i, group)
            action(index)

        start = 1 if skip_self else 0
        if group <= 16:
            for i in range(start, group):
                one(i)
        else:
            pl.loop(start, group)(one)

    half_group = group // 2
    parity = lax.rem(row, 2)
    pair = row + 1 - 2 * parity
    spot = lax.div(row, 2) * n_rad + rad

    def alike(index):
        return {
            "row": 2 * lax.div(index, n_rad) + parity,
            "rad": lax.rem(index, n_rad),
        }

    def each_alike(action, skip_self=False):
        def one(i):
            action(alike(lax.rem(spot + i, half_group)))

        start = 1 if skip_self else 0
        if group <= 16:
            for i in range(start, half_group):
                one(i)
        else:
            pl.loop(start, half_group)(one)

    def slot_of(owner):
        across, along = lax.div(owner, n_rad), lax.rem(owner, n_rad)
        return lax.rem(across, 2) * half_group + lax.div(across, 2) * n_rad + along

    def send(src, dst, send_sem, recv_sem, to):
        pltpu.make_async_remote_copy(
            src_ref=src,
            dst_ref=dst,
            send_sem=send_sem,
            recv_sem=recv_sem,
            device_id=to,
            device_id_type=MESH,
        ).start()

    def wait(ref, sem):
        pltpu.make_async_copy(ref, ref, sem).wait()

    def rows(index):
        if isinstance(index, int):
            return pl.ds(index * nr, nr)
        return pl.ds(pl.multiple_of(index * nr, nr), nr)

    loads = [
        pltpu.make_async_copy(src, dst, loaded.at[i])
        for i, (src, dst) in enumerate(
            (
                (state_hbm, state),
                (viscosity_hbm, viscosity),
                (face_circum_hbm, face_circum),
                (face_radial_hbm, face_radial),
                (weight_hbm, weight),
                (outflow_hbm, outflow),
                (volume_hbm, volume),
                (face_axial_hbm, face_axial),
                (up_hbm, up),
                (coupling_hbm, coupling),
                (matrix_hbm, matrix),
                (down_hbm, down),
            )
        )
    ]
    for load in loads:
        load.start()

    barrier = pltpu.get_barrier_semaphore()

    def greet(to):
        pl.semaphore_signal(barrier, inc=1, device_id=to, device_id_type=MESH)

    greet({"row": left})
    greet({"row": right})

    @pl.when(jnp.logical_not(floor))
    def _():
        greet({"rad": rad - 1})

    @pl.when(jnp.logical_not(casing))
    def _():
        greet({"rad": rad + 1})

    @pl.when(jnp.logical_not(first))
    def _():
        each(lambda index: greet(device(sec - 1, index)))

    @pl.when(jnp.logical_not(last))
    def _():
        each(lambda index: greet(device(sec + 1, index)))

    @pl.when(first)
    def _():
        each(lambda index: greet(device(sec, index)), True)

    @pl.when(last)
    def _():
        each(lambda index: greet(device(sec, index)), True)

    blank = jnp.zeros((nr, lanes), jnp.float32)
    for v in range(nv):
        for slot in range(2):
            field[slot, rows(v * nx)] = blank
    for step in range(STEPS):
        for part in range(1, 3):
            for side in range(2):
                rad_out0[step, part, side] = blank

    @pl.when(floor)
    def _():
        for step in range(STEPS):
            rad_in[step, 0] = jnp.zeros(rad_in.shape[2:], jnp.float32)
            for part in range(1, 3):
                rad_in0[step, part, 0] = blank

    @pl.when(casing)
    def _():
        for step in range(STEPS):
            rad_in[step, 1] = jnp.zeros(rad_in.shape[2:], jnp.float32)
            for part in range(1, 3):
                rad_in0[step, part, 1] = blank

    def pressure_of(values):
        total = weight[0] * values[0]
        for v in range(1, nv):
            total = total + weight[v] * values[v]
        return total

    def pack_one(packs, value, index):
        to_left, to_right = packs
        to_left = jnp.where(lane == index, pltpu.roll(value, index, 1), to_left)
        to_right = jnp.where(lane == index, pltpu.roll(value, index + 1, 1), to_right)
        return to_left, to_right

    def pack_start(x, packs):
        for v in range(nv):
            packs = pack_one(packs, state[rows(v * nx + x)], v * nx + x)
        packs = pack_one(packs, viscosity[rows(x)], planes + x)
        return pack_one(packs, face_circum[rows(x)], planes + nx + x)

    for load in loads[:6]:
        load.wait()
    press_send[0] = pressure_of([state[rows(v * nx)] for v in range(nv)])
    press_send[STEPS] = pressure_of([outflow[rows(v)] for v in range(nv)])
    for v in range(nv):
        flow_send[0, rows(v)] = state[rows(v * nx + nx - 1)]
    for side, edge in ((0, 0), (1, nr - 1)):
        rad_out[0, side, pl.ds(0, planes)] = state[pl.ds(edge, planes, stride=nr)]
        rad_out[0, side, pl.ds(planes, nx)] = viscosity[pl.ds(edge, nx, stride=nr)]
        rad_out[0, side, pl.ds(planes + nx, nx)] = face_radial[pl.ds(edge, nx, stride=nr)]
    packs = lax.fori_loop(0, nx, pack_start, (blank, blank), unroll=True)
    row_out[0, 0, 0] = packs[0]
    row_out[0, 0, 1] = packs[1]

    one = jnp.int32(1)
    zero = jnp.int32(0)
    inner = group + group - jnp.where(jnp.logical_or(first, last), one, zero)
    inner = inner - (1 if n_sec == 1 else 0)
    beside = jnp.where(floor, zero, one) + jnp.where(casing, zero, one)
    pl.semaphore_wait(barrier, 2 + inner + beside)

    def send_flow(step):
        @pl.when(jnp.logical_not(last))
        def _():
            each_alike(
                lambda to: send(
                    flow_send.at[step],
                    flow[step].at[parity * half_group + spot],
                    flow_ss.at[step],
                    flow_rs.at[step],
                    {"sec": sec + 1, **to},
                )
            )

    def halves(step):
        own = flow[step].at[pl.ds(parity * half_group, half_group)]
        other = flow[step].at[pl.ds((1 - parity) * half_group, half_group)]
        return own, other

    def pass_flow(step):
        def go():
            own, _ = halves(step)
            wait(own, flow_rs.at[step])
            send(own, own, pass_ss.at[step], pass_rs.at[step], {"row": pair})

        if step:
            pl.when(jnp.logical_not(first))(go)
        else:
            go()

    def send_press(step):
        @pl.when(jnp.logical_not(first))
        def _():
            each(
                lambda index: send(
                    press_send.at[step],
                    press[step].at[mine],
                    press_ss.at[step],
                    press_rs.at[step],
                    device(sec - 1, index),
                )
            )

    def send_rows(step, part):
        for side, to in ((0, left), (1, right)):
            send(
                row_out.at[step, part, side],
                row_in.at[step, part, 1 - side],
                row_ss.at[step, part, side],
                row_rs.at[step, part, 1 - side],
                {"row": to},
            )

    def rad_refs(step, part, side):
        if part:
            return rad_out0.at[step, part, side], rad_in0.at[step, part, 1 - side]
        count = planes if step else planes + 2 * nx
        return (
            rad_out.at[step, side, pl.ds(0, count)],
            rad_in.at[step, 1 - side, pl.ds(0, count)],
        )

    def send_rads(step, part):
        for side, edge, to in ((0, floor, rad - 1), (1, casing, rad + 1)):

            @pl.when(jnp.logical_not(edge))
            def _(side=side, to=to):
                src, dst = rad_refs(step, part, side)
                send(
                    src,
                    dst,
                    rad_ss.at[step, part, side],
                    rad_rs.at[step, part, 1 - side],
                    {"rad": to},
                )

    def wait_beside(step, part):
        for side, edge in ((0, floor), (1, casing)):
            wait(row_in.at[step, part, side], row_rs.at[step, part, side])

            @pl.when(jnp.logical_not(edge))
            def _(side=side):
                wait(rad_refs(step, part, 1 - side)[1], rad_rs.at[step, part, side])

    send_rows(0, 0)
    send_rads(0, 0)
    send_press(0)

    @pl.when(last)
    def _():
        each(
            lambda index: send(
                press_send.at[STEPS],
                press[0].at[mine],
                edge_ss.at[1],
                press_rs.at[0],
                device(sec, index),
            ),
            True,
        )
        pltpu.make_async_copy(press_send.at[STEPS], press[0].at[mine], press_rs.at[0]).start()

    @pl.when(first)
    def _():
        place = flow[0].at[parity * half_group + spot]
        each_alike(
            lambda to: send(inflow, place, edge_ss.at[0], flow_rs.at[0], to), True
        )
        pltpu.make_async_copy(inflow, place, flow_rs.at[0]).start()

    send_flow(0)

    def lower_lane(value, packed, index):
        return jnp.where(
            lane == 0, pltpu.roll(packed, lax.rem(lanes - index, lanes), 1), pltpu.roll(value, 1, 1)
        )

    def upper_lane(value, packed, index):
        return jnp.where(
            lane == lanes - 1,
            pltpu.roll(packed, lanes - 1 - index, 1),
            pltpu.roll(value, lanes - 1, 1),
        )

    def lower_sub(value, edge_row):
        return jnp.where(sub == 0, edge_row, pltpu.roll(value, 1, 0))

    def upper_sub(value, edge_row):
        return jnp.where(sub == nr - 1, edge_row, pltpu.roll(value, nr - 1, 0))

    wall = jnp.logical_and(casing, sub == nr - 1)

    def put_direction(x, d, half, mu, lower, upper):
        area_l, mu_l = lower
        area_u, mu_u = upper
        mix_l, mix_u = half * area_l, half * area_u
        spread_l, spread_u = mix_l * (mu_l + mu), mix_u * (mu_u + mu)
        coef[5 * d, rows(x)] = mix_u
        coef[5 * d + 1, rows(x)] = mix_u - mix_l
        coef[5 * d + 2, rows(x)] = mix_l
        coef[5 * d + 3, rows(x)] = spread_u
        coef[5 * d + 4, rows(x)] = spread_l
        return spread_l + spread_u

    def prepare_axial(x, carry):
        below, above = jnp.maximum(x - 1, 0), jnp.minimum(x + 1, nx - 1)
        half = (0.5 * time_step) / volume[rows(x)]
        lower = face_axial[rows(below)], viscosity[rows(below)]
        upper = face_axial[rows(x)], viscosity[rows(above)]
        leaves = put_direction(x, 0, half, viscosity[rows(x)], lower, upper)
        coef[N_COEF - 1, rows(x)] = 1.0 - leaves
        coef[N_COEF, rows(x)] = half
        return carry

    def prepare_beside(x, carry):
        half = coef[N_COEF, rows(x)]
        mu = viscosity[rows(x)]
        area = jnp.where(wall, 0.0, face_radial[rows(x)])
        around = face_circum[rows(x)]
        from_left, from_right = row_in[0, 0, 0], row_in[0, 0, 1]
        lower = (
            lower_sub(area, rad_in[0, 0, pl.ds(planes + nx + x, 1)]),
            lower_sub(mu, rad_in[0, 0, pl.ds(planes + x, 1)]),
        )
        upper = area, upper_sub(mu, rad_in[0, 1, pl.ds(planes + x, 1)])
        leaves = put_direction(x, 1, half, mu, lower, upper)
        lower = (
            lower_lane(around, from_left, planes + nx + x),
            lower_lane(mu, from_left, planes + x),
        )
        upper = around, upper_lane(mu, from_right, planes + x)
        leaves = leaves + put_direction(x, 2, half, mu, lower, upper)
        coef[N_COEF - 1, rows(x)] = coef[N_COEF - 1, rows(x)] - leaves
        return carry

    for load in loads[6:]:
        load.wait()
    lax.fori_loop(0, nx, prepare_axial, 0, unroll=True)
    wait_beside(0, 0)
    prepare_beside(nx - 1, 0)

    def advance(x, centre, before, after, packed, edge_rows):
        from_left, from_right = packed
        c = [coef[k, rows(x)] for k in range(N_COEF)]
        mixed, fresh = [], []
        for v in range(nv):
            index = v * nx + x
            mid = centre[v]
            below, above = edge_rows(v)
            pairs = (
                (before and before[v], after and after[v]),
                (lower_sub(mid, below), upper_sub(mid, above)),
                (lower_lane(mid, from_left, index), upper_lane(mid, from_right, index)),
            )
            kept = c[N_COEF - 1] * mid
            for d, (lo, hi) in enumerate(pairs):
                mix = c[5 * d + 1] * mid
                if hi is not None:
                    mix = mix + c[5 * d] * hi
                    kept = kept + c[5 * d + 3] * hi
                if lo is not None:
                    mix = mix - c[5 * d + 2] * lo
                    kept = kept + c[5 * d + 4] * lo
                mixed.append(mix)
            fresh.append(kept)
        result = []
        for u in range(nv):
            total = None
            for d in range(3):
                for v in range(nv):
                    term = matrix[d * nv + u, 0, v] * mixed[3 * v + d]
                    total = term if total is None else total + term
            result.append(fresh[u] - total)
        return result

    def complete(x, ghosts, mix_at, keep_at):
        mix, spread = coef[mix_at, rows(x)], coef[keep_at, rows(x)]
        mixed = [mix * ghosts[v] for v in range(nv)]
        result = []
        for u in range(nv):
            total = matrix[u, 0, 0] * mixed[0]
            for v in range(1, nv):
                total = total + matrix[u, 0, v] * mixed[v]
            if mix_at == 0:
                total = -total
            result.append((base[rows(u)] + spread * ghosts[u]) + total)
        return result

    def keep_base(values):
        for v in range(nv):
            base[rows(v)] = values[v]

    for step in range(STEPS):
        final = step == STEPS - 1
        src = state if step == 0 else field.at[(step - 1) % 2]
        dst = out if final else field.at[step % 2]
        if step:
            wait_beside(step, 0)

        def plane(x):
            return [src[rows(v * nx + x)] for v in range(nv)]

        def keep_plane(x, values):
            for v in range(nv):
                dst[rows(v * nx + x)] = values[v]

        def pack_plane(x, values, packs):
            if final:
                return packs
            for v in range(nv):
                packs = pack_one(packs, values[v], v * nx + x)
            return packs

        def edge_rows_at(x, step=step):
            def edge_rows(v):
                at = pl.ds(v * nx + x, 1)
                return rad_in[step, 0, at], rad_in[step, 1, at]

            return edge_rows

        def edge_rows_of(part, step=step):
            def edge_rows(v):
                at = pl.ds(v, 1)
                return rad_in0[step, part, 0, at], rad_in0[step, part, 1, at]

            return edge_rows

        def send_plane(part, x, values, step=step):
            packs = pack_plane(x, values, (blank, blank))
            row_out[step + 1, part, 0] = packs[0]
            row_out[step + 1, part, 1] = packs[1]
            send_rows(step + 1, part)
            for v in range(nv):
                rad_out0[step + 1, part, 0, pl.ds(v, 1)] = values[v][:1]
                rad_out0[step + 1, part, 1, pl.ds(v, 1)] = values[v][nr - 1 :]
            send_rads(step + 1, part)

        def send_inside(packs, step=step, dst=dst):
            row_out[step + 1, 0, 0] = packs[0]
            row_out[step + 1, 0, 1] = packs[1]
            send_rows(step + 1, 0)
            for side, edge in ((0, 0), (1, nr - 1)):
                rad_out[step + 1, side, pl.ds(0, planes)] = dst[pl.ds(edge, planes, stride=nr)]
            send_rads(step + 1, 0)

        def inside(x, packs):
            packed = row_in[step, 0, 0], row_in[step, 0, 1]
            values = advance(
                x, plane(x), plane(x - 1), plane(x + 1), packed, edge_rows_at(x)
            )
            keep_plane(x, values)
            return pack_plane(x, values, packs)

        def all_inside(packs):
            return lax.fori_loop(1, nx - 1, inside, packs, unroll=True)

        packs = blank, blank
        if step:
            packs = all_inside(packs)
            if not final:
                send_inside(packs)

        centre = plane(nx - 1)
        if step:
            wait_beside(step, 2)
            edge_rows = edge_rows_of(2)
            packed = row_in[step, 2, 0], row_in[step, 2, 1]
        else:
            edge_rows = edge_rows_at(nx - 1)
            packed = row_in[0, 0, 0], row_in[0, 0, 1]
        keep_base(advance(nx - 1, centre, plane(nx - 2), None, packed, edge_rows))
        if step:
            pass_flow(step)

        def take_press(step=step):
            donors = [up[0, a] for a in range(nr)]
            spots = [(lax.div(donor, nr), lax.rem(donor, nr)) for donor in donors]
            wait(press[step], press_rs.at[step])
            for a, (owner, at) in enumerate(spots):
                mapped[pl.ds(a, 1)] = press[step][owner, pl.ds(at, 1)]

        if step:
            pl.when(jnp.logical_not(last))(take_press)
        else:
            take_press()
        centre = plane(nx - 1)
        gap = mapped[...] - pressure_of(centre)
        after = [centre[v] + coupling[v] * gap for v in range(nv)]
        values = complete(nx - 1, after, 0, 3)
        keep_plane(nx - 1, values)
        if not final:
            for v in range(nv):
                flow_send[step + 1, rows(v)] = values[v]
            send_flow(step + 1)
        if step == 0:
            pass_flow(0)
            lax.fori_loop(0, nx - 1, prepare_beside, 0, unroll=True)
            send_inside(all_inside(packs))
        if not final:
            send_plane(2, nx - 1, values)

        def take_flow(step=step):
            donors = [down[0, a] for a in range(nr)]
            spots = [
                (slot_of(lax.div(donor, nr)), lax.rem(donor, nr)) for donor in donors
            ]
            wait(halves(step)[1], pass_rs.at[step])
            for a, (owner, at) in enumerate(spots):
                for v in range(nv):
                    ghost[pl.ds(v * nr + a, 1)] = flow[step][owner, pl.ds(v * nr + at, 1)]

        if step:
            wait_beside(step, 1)

            edge_rows = edge_rows_of(1)
            packed = row_in[step, 1, 0], row_in[step, 1, 1]
        else:
            edge_rows = edge_rows_at(0)
        keep_base(advance(0, plane(0), None, plane(1), packed, edge_rows))
        if step:
            pl.when(jnp.logical_not(first))(take_flow)
        else:
            take_flow()
        values = complete(0, [ghost[rows(v)] for v in range(nv)], 2, 4)
        keep_plane(0, values)
        if not final:
            press_send[step + 1] = pressure_of(values)
            send_press(step + 1)
            send_plane(1, 0, values)

    wait(halves(0)[0], pass_ss.at[0])

    @pl.when(jnp.logical_not(first))
    def _():
        for step in range(1, STEPS):
            wait(halves(step)[0], pass_ss.at[step])

    for step in range(STEPS):
        for part in range(3 if step else 1):
            for side, edge in ((0, floor), (1, casing)):
                wait(row_out.at[step, part, side], row_ss.at[step, part, side])

                @pl.when(jnp.logical_not(edge))
                def _(step=step, part=part, side=side):
                    wait(rad_refs(step, part, side)[0], rad_ss.at[step, part, side])

    @pl.when(jnp.logical_not(last))
    def _():
        for step in range(STEPS):
            wait(flow[step].at[pl.ds(0, half_group)], flow_ss.at[step])

    @pl.when(jnp.logical_not(first))
    def _():
        for step in range(STEPS):
            wait(press[step], press_ss.at[step])

    @pl.when(first)
    def _():
        wait(flow[0].at[pl.ds(0, half_group - 1)], edge_ss.at[0])

    @pl.when(last)
    def _():
        wait(press[0].at[pl.ds(0, group - 1)], edge_ss.at[1])


def body(
    n_sec,
    n_row,
    n_rad,
    state,
    volume,
    face_axial,
    face_radial,
    face_circum,
    viscosity,
    flux_matrix,
    inflow_plane,
    outflow_plane,
    down_donors,
    up_donors,
    pressure_weight,
    boundary_coupling,
):
    nv, _, nx, nr, lanes = state.shape
    group = n_row * n_rad
    planes, block = nv * nx, nv * nr
    held = planes + 2 * nx

    def flat(array):
        return array.reshape(-1, lanes)

    def vmem(*shape):
        return pltpu.VMEM(shape, jnp.float32)

    dma = pltpu.SemaphoreType.DMA
    in_vmem = pl.BlockSpec(memory_space=pltpu.VMEM)
    result = pl.pallas_call(
        functools.partial(kernel, (n_sec, n_row, n_rad, nv, nx, nr, lanes)),
        out_shape=pltpu.VMEM((planes * nr, lanes), jnp.float32),
        in_specs=[pl.BlockSpec(memory_space=pltpu.HBM)] * 13,
        out_specs=in_vmem,
        scratch_shapes=[
            vmem(planes * nr, lanes),
            *[vmem(nx * nr, lanes)] * 5,
            pltpu.SMEM((3 * nv, 1, nv), jnp.float32),
            vmem(block, lanes),
            pltpu.SMEM(down_donors.shape, jnp.int32),
            pltpu.SMEM(up_donors.shape, jnp.int32),
            pltpu.SMEM(pressure_weight.shape, jnp.float32),
            pltpu.SMEM(boundary_coupling.shape, jnp.float32),
            dma((12,)),
            vmem(2, planes * nr, lanes),
            vmem(N_COEF + 1, nx * nr, lanes),
            [vmem(group, block, lanes)] * STEPS,
            vmem(STEPS, block, lanes),
            [vmem(group, nr, lanes)] * STEPS,
            vmem(STEPS + 1, nr, lanes),
            vmem(block, lanes),
            vmem(nr, lanes),
            vmem(block, lanes),
            vmem(STEPS, 3, 2, nr, lanes),
            vmem(STEPS, 3, 2, nr, lanes),
            vmem(STEPS, 2, held, lanes),
            vmem(STEPS, 2, held, lanes),
            vmem(STEPS, 3, 2, nr, lanes),
            vmem(STEPS, 3, 2, nr, lanes),
            dma((STEPS,)),
            dma((STEPS,)),
            dma((STEPS,)),
            dma((STEPS,)),
            dma((STEPS,)),
            dma((STEPS,)),
            dma((2,)),
            dma((STEPS, 3, 2)),
            dma((STEPS, 3, 2)),
            dma((STEPS, 3, 2)),
            dma((STEPS, 3, 2)),
        ],
        compiler_params=pltpu.CompilerParams(
            collective_id=0, has_side_effects=True, vmem_limit_bytes=60 * 1024 * 1024
        ),
        name="coupled_steps",
    )(
        flat(state),
        flat(volume),
        flat(face_axial),
        flat(face_radial),
        flat(face_circum),
        flat(viscosity),
        flux_matrix.transpose(1, 2, 0, 3).reshape(3 * nv, 1, nv),
        flat(inflow_plane),
        flat(outflow_plane),
        down_donors,
        up_donors,
        pressure_weight,
        boundary_coupling,
    )
    return result.reshape(state.shape)


def solution(mesh):
    in_specs = (
        P(None, "sec", None, "rad", "row"),
        P("sec", None, "rad", "row"),
        P("sec", None, "rad", "row"),
        P("sec", None, "rad", "row"),
        P("sec", None, "rad", "row"),
        P("sec", None, "rad", "row"),
        P("sec", None, None, None),
        P(None, "rad", "row"),
        P(None, "rad", "row"),
        P("sec", ("row", "rad")),
        P("sec", ("row", "rad")),
        P(),
        P(),
    )
    out_specs = P(None, "sec", None, "rad", "row")
    sizes = tuple(mesh.shape[name] for name in ("sec", "row", "rad"))
    return jax.shard_map(
        functools.partial(body, *sizes),
        mesh=mesh,
        in_specs=in_specs,
        out_specs=out_specs,
        check_vma=False,
    )
```

```python
import functools

import jax
import jax.numpy as jnp
from jax import lax
from jax.experimental import pallas as pl
from jax.experimental.pallas import tpu as pltpu
from jax.sharding import PartitionSpec as P

STEPS = 4


time_step = 0.08

MESH = pl.DeviceIdType.MESH
N_COEF = 16


def kernel(
    sizes,
    state_hbm,
    volume_hbm,
    face_axial_hbm,
    face_radial_hbm,
    face_circum_hbm,
    viscosity_hbm,
    matrix_hbm,
    inflow,
    outflow_hbm,
    down_hbm,
    up_hbm,
    weight_hbm,
    coupling_hbm,
    out,
    state,
    volume,
    face_axial,
    face_radial,
    face_circum,
    viscosity,
    matrix,
    outflow,
    down,
    up,
    weight,
    coupling,
    loaded,
    field,
    coef,
    flow,
    flow_send,
    press,
    press_send,
    ghost,
    mapped,
    base,
    row_in,
    row_out,
    rad_in,
    rad_out,
    rad_in0,
    rad_out0,
    flow_ss,
    flow_rs,
    pass_ss,
    pass_rs,
    press_ss,
    press_rs,
    edge_ss,
    row_ss,
    row_rs,
    rad_ss,
    rad_rs,
):
    n_sec, n_row, n_rad, nv, nx, nr, lanes = sizes
    group = n_row * n_rad
    planes = nv * nx
    sec, row, rad = lax.axis_index("sec"), lax.axis_index("row"), lax.axis_index("rad")
    mine = row * n_rad + rad
    first, last = sec == 0, sec == n_sec - 1
    floor, casing = rad == 0, rad == n_rad - 1
    right, left = lax.rem(row + 1, n_row), lax.rem(row + n_row - 1, n_row)
    lane = lax.broadcasted_iota(jnp.int32, (nr, lanes), 1)
    sub = lax.broadcasted_iota(jnp.int32, (nr, lanes), 0)

    def device(section, index):
        return {"sec": section, "row": lax.div(index, n_rad), "rad": lax.rem(index, n_rad)}

    def each(action, skip_self=False):
        def one(i):
            index = lax.rem(mine + i, group)
            action(index)

        start = 1 if skip_self else 0
        if group <= 16:
            for i in range(start, group):
                one(i)
        else:
            pl.loop(start, group)(one)

    half_group = group // 2
    parity = lax.rem(row, 2)
    pair = row + 1 - 2 * parity
    spot = lax.div(row, 2) * n_rad + rad

    def alike(index):
        return {
            "row": 2 * lax.div(index, n_rad) + parity,
            "rad": lax.rem(index, n_rad),
        }

    def each_alike(action, skip_self=False):
        def one(i):
            action(alike(lax.rem(spot + i, half_group)))

        start = 1 if skip_self else 0
        if group <= 16:
            for i in range(start, half_group):
                one(i)
        else:
            pl.loop(start, half_group)(one)

    def slot_of(owner):
        across, along = lax.div(owner, n_rad), lax.rem(owner, n_rad)
        return lax.rem(across, 2) * half_group + lax.div(across, 2) * n_rad + along

    def send(src, dst, send_sem, recv_sem, to):
        pltpu.make_async_remote_copy(
            src_ref=src,
            dst_ref=dst,
            send_sem=send_sem,
            recv_sem=recv_sem,
            device_id=to,
            device_id_type=MESH,
        ).start()

    def wait(ref, sem):
        pltpu.make_async_copy(ref, ref, sem).wait()

    def rows(index):
        if isinstance(index, int):
            return pl.ds(index * nr, nr)
        return pl.ds(pl.multiple_of(index * nr, nr), nr)

    loads = [
        pltpu.make_async_copy(src, dst, loaded.at[i])
        for i, (src, dst) in enumerate(
            (
                (state_hbm, state),
                (viscosity_hbm, viscosity),
                (face_circum_hbm, face_circum),
                (face_radial_hbm, face_radial),
                (weight_hbm, weight),
                (outflow_hbm, outflow),
                (volume_hbm, volume),
                (face_axial_hbm, face_axial),
                (up_hbm, up),
                (coupling_hbm, coupling),
                (matrix_hbm, matrix),
                (down_hbm, down),
            )
        )
    ]
    for load in loads:
        load.start()

    barrier = pltpu.get_barrier_semaphore()

    def greet(to):
        pl.semaphore_signal(barrier, inc=1, device_id=to, device_id_type=MESH)

    greet({"row": left})
    greet({"row": right})

    @pl.when(jnp.logical_not(floor))
    def _():
        greet({"rad": rad - 1})

    @pl.when(jnp.logical_not(casing))
    def _():
        greet({"rad": rad + 1})

    @pl.when(jnp.logical_not(first))
    def _():
        each(lambda index: greet(device(sec - 1, index)))

    @pl.when(jnp.logical_not(last))
    def _():
        each(lambda index: greet(device(sec + 1, index)))

    @pl.when(first)
    def _():
        each(lambda index: greet(device(sec, index)), True)

    @pl.when(last)
    def _():
        each(lambda index: greet(device(sec, index)), True)

    blank = jnp.zeros((nr, lanes), jnp.float32)
    for v in range(nv):
        for slot in range(2):
            field[slot, rows(v * nx)] = blank
    for step in range(STEPS):
        for part in range(1, 3):
            for side in range(2):
                rad_out0[step, part, side] = blank

    @pl.when(floor)
    def _():
        for step in range(STEPS):
            rad_in[step, 0] = jnp.zeros(rad_in.shape[2:], jnp.float32)
            for part in range(1, 3):
                rad_in0[step, part, 0] = blank

    @pl.when(casing)
    def _():
        for step in range(STEPS):
            rad_in[step, 1] = jnp.zeros(rad_in.shape[2:], jnp.float32)
            for part in range(1, 3):
                rad_in0[step, part, 1] = blank

    def pressure_of(values):
        total = weight[0] * values[0]
        for v in range(1, nv):
            total = total + weight[v] * values[v]
        return total

    def pack_one(packs, value, index):
        to_left, to_right = packs
        to_left = jnp.where(lane == index, pltpu.roll(value, index, 1), to_left)
        to_right = jnp.where(lane == index, pltpu.roll(value, index + 1, 1), to_right)
        return to_left, to_right

    def pack_start(x, packs):
        for v in range(nv):
            packs = pack_one(packs, state[rows(v * nx + x)], v * nx + x)
        packs = pack_one(packs, viscosity[rows(x)], planes + x)
        return pack_one(packs, face_circum[rows(x)], planes + nx + x)

    for load in loads[:6]:
        load.wait()
    press_send[0] = pressure_of([state[rows(v * nx)] for v in range(nv)])
    press_send[STEPS] = pressure_of([outflow[rows(v)] for v in range(nv)])
    for v in range(nv):
        flow_send[0, rows(v)] = state[rows(v * nx + nx - 1)]
    for side, edge in ((0, 0), (1, nr - 1)):
        rad_out[0, side, pl.ds(0, planes)] = state[pl.ds(edge, planes, stride=nr)]
        rad_out[0, side, pl.ds(planes, nx)] = viscosity[pl.ds(edge, nx, stride=nr)]
        rad_out[0, side, pl.ds(planes + nx, nx)] = face_radial[pl.ds(edge, nx, stride=nr)]
    packs = lax.fori_loop(0, nx, pack_start, (blank, blank), unroll=4)
    row_out[0, 0, 0] = packs[0]
    row_out[0, 0, 1] = packs[1]

    one = jnp.int32(1)
    zero = jnp.int32(0)
    inner = group + group - jnp.where(jnp.logical_or(first, last), one, zero)
    inner = inner - (1 if n_sec == 1 else 0)
    beside = jnp.where(floor, zero, one) + jnp.where(casing, zero, one)
    pl.semaphore_wait(barrier, 2 + inner + beside)

    def send_flow(step):
        @pl.when(jnp.logical_not(last))
        def _():
            each_alike(
                lambda to: send(
                    flow_send.at[step],
                    flow[step].at[parity * half_group + spot],
                    flow_ss.at[step],
                    flow_rs.at[step],
                    {"sec": sec + 1, **to},
                )
            )

    def halves(step):
        own = flow[step].at[pl.ds(parity * half_group, half_group)]
        other = flow[step].at[pl.ds((1 - parity) * half_group, half_group)]
        return own, other

    def pass_flow(step):
        def go():
            own, _ = halves(step)
            wait(own, flow_rs.at[step])
            send(own, own, pass_ss.at[step], pass_rs.at[step], {"row": pair})

        if step:
            pl.when(jnp.logical_not(first))(go)
        else:
            go()

    def send_press(step):
        @pl.when(jnp.logical_not(first))
        def _():
            each(
                lambda index: send(
                    press_send.at[step],
                    press[step].at[mine],
                    press_ss.at[step],
                    press_rs.at[step],
                    device(sec - 1, index),
                )
            )

    def send_rows(step, part):
        for side, to in ((0, left), (1, right)):
            send(
                row_out.at[step, part, side],
                row_in.at[step, part, 1 - side],
                row_ss.at[step, part, side],
                row_rs.at[step, part, 1 - side],
                {"row": to},
            )

    def rad_refs(step, part, side):
        if part:
            return rad_out0.at[step, part, side], rad_in0.at[step, part, 1 - side]
        count = planes if step else planes + 2 * nx
        return (
            rad_out.at[step, side, pl.ds(0, count)],
            rad_in.at[step, 1 - side, pl.ds(0, count)],
        )

    def send_rads(step, part):
        for side, edge, to in ((0, floor, rad - 1), (1, casing, rad + 1)):

            @pl.when(jnp.logical_not(edge))
            def _(side=side, to=to):
                src, dst = rad_refs(step, part, side)
                send(
                    src,
                    dst,
                    rad_ss.at[step, part, side],
                    rad_rs.at[step, part, 1 - side],
                    {"rad": to},
                )

    def wait_beside(step, part):
        for side, edge in ((0, floor), (1, casing)):
            wait(row_in.at[step, part, side], row_rs.at[step, part, side])

            @pl.when(jnp.logical_not(edge))
            def _(side=side):
                wait(rad_refs(step, part, 1 - side)[1], rad_rs.at[step, part, side])

    send_rows(0, 0)
    send_rads(0, 0)
    send_press(0)

    @pl.when(last)
    def _():
        each(
            lambda index: send(
                press_send.at[STEPS],
                press[0].at[mine],
                edge_ss.at[1],
                press_rs.at[0],
                device(sec, index),
            ),
            True,
        )
        pltpu.make_async_copy(press_send.at[STEPS], press[0].at[mine], press_rs.at[0]).start()

    @pl.when(first)
    def _():
        place = flow[0].at[parity * half_group + spot]
        each_alike(
            lambda to: send(inflow, place, edge_ss.at[0], flow_rs.at[0], to), True
        )
        pltpu.make_async_copy(inflow, place, flow_rs.at[0]).start()

    send_flow(0)

    def lower_lane(value, packed, index):
        return jnp.where(
            lane == 0, pltpu.roll(packed, lax.rem(lanes - index, lanes), 1), pltpu.roll(value, 1, 1)
        )

    def upper_lane(value, packed, index):
        return jnp.where(
            lane == lanes - 1,
            pltpu.roll(packed, lanes - 1 - index, 1),
            pltpu.roll(value, lanes - 1, 1),
        )

    def lower_sub(value, edge_row):
        return jnp.where(sub == 0, edge_row, pltpu.roll(value, 1, 0))

    def upper_sub(value, edge_row):
        return jnp.where(sub == nr - 1, edge_row, pltpu.roll(value, nr - 1, 0))

    wall = jnp.logical_and(casing, sub == nr - 1)

    def put_direction(x, d, half, mu, lower, upper):
        area_l, mu_l = lower
        area_u, mu_u = upper
        mix_l, mix_u = half * area_l, half * area_u
        spread_l, spread_u = mix_l * (mu_l + mu), mix_u * (mu_u + mu)
        coef[5 * d, rows(x)] = mix_u
        coef[5 * d + 1, rows(x)] = mix_u - mix_l
        coef[5 * d + 2, rows(x)] = mix_l
        coef[5 * d + 3, rows(x)] = spread_u
        coef[5 * d + 4, rows(x)] = spread_l
        return spread_l + spread_u

    def prepare_axial(x, carry):
        below, above = jnp.maximum(x - 1, 0), jnp.minimum(x + 1, nx - 1)
        half = (0.5 * time_step) / volume[rows(x)]
        lower = face_axial[rows(below)], viscosity[rows(below)]
        upper = face_axial[rows(x)], viscosity[rows(above)]
        leaves = put_direction(x, 0, half, viscosity[rows(x)], lower, upper)
        coef[N_COEF - 1, rows(x)] = 1.0 - leaves
        coef[N_COEF, rows(x)] = half
        return carry

    def prepare_beside(x, carry):
        half = coef[N_COEF, rows(x)]
        mu = viscosity[rows(x)]
        area = jnp.where(wall, 0.0, face_radial[rows(x)])
        around = face_circum[rows(x)]
        from_left, from_right = row_in[0, 0, 0], row_in[0, 0, 1]
        lower = (
            lower_sub(area, rad_in[0, 0, pl.ds(planes + nx + x, 1)]),
            lower_sub(mu, rad_in[0, 0, pl.ds(planes + x, 1)]),
        )
        upper = area, upper_sub(mu, rad_in[0, 1, pl.ds(planes + x, 1)])
        leaves = put_direction(x, 1, half, mu, lower, upper)
        lower = (
            lower_lane(around, from_left, planes + nx + x),
            lower_lane(mu, from_left, planes + x),
        )
        upper = around, upper_lane(mu, from_right, planes + x)
        leaves = leaves + put_direction(x, 2, half, mu, lower, upper)
        coef[N_COEF - 1, rows(x)] = coef[N_COEF - 1, rows(x)] - leaves
        return carry

    for load in loads[6:]:
        load.wait()
    lax.fori_loop(0, nx, prepare_axial, 0, unroll=4)
    wait_beside(0, 0)
    prepare_beside(nx - 1, 0)

    def advance(x, centre, before, after, packed, edge_rows):
        from_left, from_right = packed
        c = [coef[k, rows(x)] for k in range(N_COEF)]
        mixed, fresh = [], []
        for v in range(nv):
            index = v * nx + x
            mid = centre[v]
            below, above = edge_rows(v)
            pairs = (
                (before and before[v], after and after[v]),
                (lower_sub(mid, below), upper_sub(mid, above)),
                (lower_lane(mid, from_left, index), upper_lane(mid, from_right, index)),
            )
            kept = c[N_COEF - 1] * mid
            for d, (lo, hi) in enumerate(pairs):
                mix = c[5 * d + 1] * mid
                if hi is not None:
                    mix = mix + c[5 * d] * hi
                    kept = kept + c[5 * d + 3] * hi
                if lo is not None:
                    mix = mix - c[5 * d + 2] * lo
                    kept = kept + c[5 * d + 4] * lo
                mixed.append(mix)
            fresh.append(kept)
        result = []
        for u in range(nv):
            total = None
            for d in range(3):
                for v in range(nv):
                    term = matrix[d * nv + u, 0, v] * mixed[3 * v + d]
                    total = term if total is None else total + term
            result.append(fresh[u] - total)
        return result

    def complete(x, ghosts, mix_at, keep_at):
        mix, spread = coef[mix_at, rows(x)], coef[keep_at, rows(x)]
        mixed = [mix * ghosts[v] for v in range(nv)]
        result = []
        for u in range(nv):
            total = matrix[u, 0, 0] * mixed[0]
            for v in range(1, nv):
                total = total + matrix[u, 0, v] * mixed[v]
            if mix_at == 0:
                total = -total
            result.append((base[rows(u)] + spread * ghosts[u]) + total)
        return result

    def keep_base(values):
        for v in range(nv):
            base[rows(v)] = values[v]

    for step in range(STEPS):
        final = step == STEPS - 1
        src = state if step == 0 else field.at[(step - 1) % 2]
        dst = out if final else field.at[step % 2]
        if step:
            wait_beside(step, 0)

        def plane(x):
            return [src[rows(v * nx + x)] for v in range(nv)]

        def keep_plane(x, values):
            for v in range(nv):
                dst[rows(v * nx + x)] = values[v]

        def pack_plane(x, values, packs):
            if final:
                return packs
            for v in range(nv):
                packs = pack_one(packs, values[v], v * nx + x)
            return packs

        def edge_rows_at(x, step=step):
            def edge_rows(v):
                at = pl.ds(v * nx + x, 1)
                return rad_in[step, 0, at], rad_in[step, 1, at]

            return edge_rows

        def edge_rows_of(part, step=step):
            def edge_rows(v):
                at = pl.ds(v, 1)
                return rad_in0[step, part, 0, at], rad_in0[step, part, 1, at]

            return edge_rows

        def send_plane(part, x, values, step=step):
            packs = pack_plane(x, values, (blank, blank))
            row_out[step + 1, part, 0] = packs[0]
            row_out[step + 1, part, 1] = packs[1]
            send_rows(step + 1, part)
            for v in range(nv):
                rad_out0[step + 1, part, 0, pl.ds(v, 1)] = values[v][:1]
                rad_out0[step + 1, part, 1, pl.ds(v, 1)] = values[v][nr - 1 :]
            send_rads(step + 1, part)

        def send_inside(packs, step=step, dst=dst):
            row_out[step + 1, 0, 0] = packs[0]
            row_out[step + 1, 0, 1] = packs[1]
            send_rows(step + 1, 0)
            for side, edge in ((0, 0), (1, nr - 1)):
                rad_out[step + 1, side, pl.ds(0, planes)] = dst[pl.ds(edge, planes, stride=nr)]
            send_rads(step + 1, 0)

        def inside(x, packs):
            packed = row_in[step, 0, 0], row_in[step, 0, 1]
            values = advance(
                x, plane(x), plane(x - 1), plane(x + 1), packed, edge_rows_at(x)
            )
            keep_plane(x, values)
            return pack_plane(x, values, packs)

        def all_inside(packs):
            return lax.fori_loop(1, nx - 1, inside, packs, unroll=max(1, (nx - 2) // 2))

        packs = blank, blank
        if step:
            packs = all_inside(packs)
            if not final:
                send_inside(packs)

        centre = plane(nx - 1)
        if step:
            wait_beside(step, 2)
            edge_rows = edge_rows_of(2)
            packed = row_in[step, 2, 0], row_in[step, 2, 1]
        else:
            edge_rows = edge_rows_at(nx - 1)
            packed = row_in[0, 0, 0], row_in[0, 0, 1]
        keep_base(advance(nx - 1, centre, plane(nx - 2), None, packed, edge_rows))
        if step:
            pass_flow(step)

        def take_press(step=step):
            donors = [up[0, a] for a in range(nr)]
            spots = [(lax.div(donor, nr), lax.rem(donor, nr)) for donor in donors]
            wait(press[step], press_rs.at[step])
            for a, (owner, at) in enumerate(spots):
                mapped[pl.ds(a, 1)] = press[step][owner, pl.ds(at, 1)]

        if step:
            pl.when(jnp.logical_not(last))(take_press)
        else:
            take_press()
        centre = plane(nx - 1)
        gap = mapped[...] - pressure_of(centre)
        after = [centre[v] + coupling[v] * gap for v in range(nv)]
        values = complete(nx - 1, after, 0, 3)
        keep_plane(nx - 1, values)
        if not final:
            for v in range(nv):
                flow_send[step + 1, rows(v)] = values[v]
            send_flow(step + 1)
        if step == 0:
            pass_flow(0)
            lax.fori_loop(0, nx - 1, prepare_beside, 0, unroll=5)
            send_inside(all_inside(packs))
        if not final:
            send_plane(2, nx - 1, values)

        def take_flow(step=step):
            donors = [down[0, a] for a in range(nr)]
            spots = [
                (slot_of(lax.div(donor, nr)), lax.rem(donor, nr)) for donor in donors
            ]
            wait(halves(step)[1], pass_rs.at[step])
            for a, (owner, at) in enumerate(spots):
                for v in range(nv):
                    ghost[pl.ds(v * nr + a, 1)] = flow[step][owner, pl.ds(v * nr + at, 1)]

        if step:
            wait_beside(step, 1)

            edge_rows = edge_rows_of(1)
            packed = row_in[step, 1, 0], row_in[step, 1, 1]
        else:
            edge_rows = edge_rows_at(0)
        keep_base(advance(0, plane(0), None, plane(1), packed, edge_rows))
        if step:
            pl.when(jnp.logical_not(first))(take_flow)
        else:
            take_flow()
        values = complete(0, [ghost[rows(v)] for v in range(nv)], 2, 4)
        keep_plane(0, values)
        if not final:
            press_send[step + 1] = pressure_of(values)
            send_press(step + 1)
            send_plane(1, 0, values)

    wait(halves(0)[0], pass_ss.at[0])

    @pl.when(jnp.logical_not(first))
    def _():
        for step in range(1, STEPS):
            wait(halves(step)[0], pass_ss.at[step])

    for step in range(STEPS):
        for part in range(3 if step else 1):
            for side, edge in ((0, floor), (1, casing)):
                wait(row_out.at[step, part, side], row_ss.at[step, part, side])

                @pl.when(jnp.logical_not(edge))
                def _(step=step, part=part, side=side):
                    wait(rad_refs(step, part, side)[0], rad_ss.at[step, part, side])

    @pl.when(jnp.logical_not(last))
    def _():
        for step in range(STEPS):
            wait(flow[step].at[pl.ds(0, half_group)], flow_ss.at[step])

    @pl.when(jnp.logical_not(first))
    def _():
        for step in range(STEPS):
            wait(press[step], press_ss.at[step])

    @pl.when(first)
    def _():
        wait(flow[0].at[pl.ds(0, half_group - 1)], edge_ss.at[0])

    @pl.when(last)
    def _():
        wait(press[0].at[pl.ds(0, group - 1)], edge_ss.at[1])


def body(
    n_sec,
    n_row,
    n_rad,
    state,
    volume,
    face_axial,
    face_radial,
    face_circum,
    viscosity,
    flux_matrix,
    inflow_plane,
    outflow_plane,
    down_donors,
    up_donors,
    pressure_weight,
    boundary_coupling,
):
    nv, _, nx, nr, lanes = state.shape
    group = n_row * n_rad
    planes, block = nv * nx, nv * nr
    held = planes + 2 * nx

    def flat(array):
        return array.reshape(-1, lanes)

    def vmem(*shape):
        return pltpu.VMEM(shape, jnp.float32)

    dma = pltpu.SemaphoreType.DMA
    in_vmem = pl.BlockSpec(memory_space=pltpu.VMEM)
    result = pl.pallas_call(
        functools.partial(kernel, (n_sec, n_row, n_rad, nv, nx, nr, lanes)),
        out_shape=pltpu.VMEM((planes * nr, lanes), jnp.float32),
        in_specs=[pl.BlockSpec(memory_space=pltpu.HBM)] * 13,
        out_specs=in_vmem,
        scratch_shapes=[
            vmem(planes * nr, lanes),
            *[vmem(nx * nr, lanes)] * 5,
            pltpu.SMEM((3 * nv, 1, nv), jnp.float32),
            vmem(block, lanes),
            pltpu.SMEM(down_donors.shape, jnp.int32),
            pltpu.SMEM(up_donors.shape, jnp.int32),
            pltpu.SMEM(pressure_weight.shape, jnp.float32),
            pltpu.SMEM(boundary_coupling.shape, jnp.float32),
            dma((12,)),
            vmem(2, planes * nr, lanes),
            vmem(N_COEF + 1, nx * nr, lanes),
            [vmem(group, block, lanes)] * STEPS,
            vmem(STEPS, block, lanes),
            [vmem(group, nr, lanes)] * STEPS,
            vmem(STEPS + 1, nr, lanes),
            vmem(block, lanes),
            vmem(nr, lanes),
            vmem(block, lanes),
            vmem(STEPS, 3, 2, nr, lanes),
            vmem(STEPS, 3, 2, nr, lanes),
            vmem(STEPS, 2, held, lanes),
            vmem(STEPS, 2, held, lanes),
            vmem(STEPS, 3, 2, nr, lanes),
            vmem(STEPS, 3, 2, nr, lanes),
            dma((STEPS,)),
            dma((STEPS,)),
            dma((STEPS,)),
            dma((STEPS,)),
            dma((STEPS,)),
            dma((STEPS,)),
            dma((2,)),
            dma((STEPS, 3, 2)),
            dma((STEPS, 3, 2)),
            dma((STEPS, 3, 2)),
            dma((STEPS, 3, 2)),
        ],
        compiler_params=pltpu.CompilerParams(
            collective_id=0, has_side_effects=True, vmem_limit_bytes=60 * 1024 * 1024
        ),
        name="coupled_steps",
    )(
        flat(state),
        flat(volume),
        flat(face_axial),
        flat(face_radial),
        flat(face_circum),
        flat(viscosity),
        flux_matrix.transpose(1, 2, 0, 3).reshape(3 * nv, 1, nv),
        flat(inflow_plane),
        flat(outflow_plane),
        down_donors,
        up_donors,
        pressure_weight,
        boundary_coupling,
    )
    return result.reshape(state.shape)


def solution(mesh):
    in_specs = (
        P(None, "sec", None, "rad", "row"),
        P("sec", None, "rad", "row"),
        P("sec", None, "rad", "row"),
        P("sec", None, "rad", "row"),
        P("sec", None, "rad", "row"),
        P("sec", None, "rad", "row"),
        P("sec", None, None, None),
        P(None, "rad", "row"),
        P(None, "rad", "row"),
        P("sec", ("row", "rad")),
        P("sec", ("row", "rad")),
        P(),
        P(),
    )
    out_specs = P(None, "sec", None, "rad", "row")
    sizes = tuple(mesh.shape[name] for name in ("sec", "row", "rad"))
    return jax.shard_map(
        functools.partial(body, *sizes),
        mesh=mesh,
        in_specs=in_specs,
        out_specs=out_specs,
        check_vma=False,
    )
```
